512 devices in a mesh: delay: 64 (over y, z_hi, core), dom: 8 (over x, z_lo).
Axes of the slice: x: 4, y: 8, z: 8 (z_hi: 4, z_lo: 2; z = z_hi * 2 + z_lo), core: 2. Of those that a mesh axis runs over, the one named last changes fastest.
Arguments:
- excitation: float32 [2, 4096, 128], P(None, 'dom', 'delay'), may hold values from -6 to 6
- retarded: bfloat16 [128, 4096, 512], P('delay', 'dom'), may hold values from -0.0234375 to 0.0234375
- history: bfloat16 [128, 4096, 128], P('delay', 'dom'), may hold values from -16 to 16
- inverse: bfloat16 [4096, 512], P('dom'), may hold values from -0.25 to 0.25
- transfer: bfloat16 [4096, 256], P('dom'), may hold values from -0.375 to 0.375
- faces: int32 [8, 256], P('dom'), may hold values from 0 to 511
- counts: int32 [8], P('dom'), may hold values from 64 to 128, as said below
Outputs:
- currents: float32 [2, 4096, 128], P(None, 'dom', 'delay')
- new_history: bfloat16 [128, 4096, 128], P('delay', 'dom')
The draws below stay inside these ranges and needn't reach their ends.
Inputs may be any that keep to these rules, and one draw needn't show every extreme that they name: `faces`: each entry names an unknown of the domain's own cluster. `counts`: at least one domain couples through all 128 delays.
All inputs are finite; a program needn't handle non-finite values.
Results may differ from the reference program's by a relative error of at most 0.006.
Values may be sent and summed in bfloat16 or wider, within the bound.
No kernel may reach another device: no remote copies, remote signals or barrier semaphores. Data moves between devices by JAX's collectives and lax.ppermute only.
A program may use at most 64 MiB of HBM per device.

```python
import jax
import jax.numpy as jnp
from jax import lax

C = 512
M = 128
STEPS = 2
EXC = 128
DOMAINS = 8
DELAYS = 128
UNKNOWNS = 4096


def draw_counts(key, part):
    key_base = jax.random.fold_in(key, 11)
    key_full = jax.random.fold_in(key, 12)
    counts_drawn = jax.random.randint(key_base, (DOMAINS,), DELAYS // 2, DELAYS + 1)
    full_at = jax.random.randint(key_full, (), 0, DOMAINS)
    return jnp.where(jnp.arange(DOMAINS) == full_at, DELAYS, counts_drawn).astype(jnp.int32)


def plant(entries, rng, smallest, largest):
    dims = entries.shape
    place = [jax.random.randint(jax.random.fold_in(rng, axis), (), 0, dims[axis]) for axis in range(len(dims))]
    entries = entries.at[tuple(place)].set(smallest)
    longest = dims.index(max(dims))
    place[longest] = (place[longest] + 1) % dims[longest]
    return entries.at[tuple(place)].set(largest)


def with_spikes(array, key, source, target, shards_of, factor):
    def block_of(position):
        return (jnp.arange(array.shape[position]) // (array.shape[position] // shards_of)).reshape((-1,) + (1,) * (array.ndim - 1 - position))

    one_side = jax.random.permutation(key, shards_of)[block_of(target)]
    other_side = (block_of(target) + shards_of // 2) % shards_of
    return jnp.where((block_of(source) == one_side) | (block_of(source) == other_side), factor * array, array)


def block_levels(key, extent, split, least, top_value):
    def one(axis_at, blocks):
        draws = jax.random.uniform(jax.random.fold_in(jax.random.fold_in(key, 6), axis_at), (blocks,), jnp.float32, least / len(split), top_value / len(split))
        return jnp.repeat(jnp.exp(draws), extent[axis_at] // blocks).reshape((-1,) + (1,) * (len(extent) - axis_at - 1))

    factor_of = one(*split[0])
    for cut in split[1:]:
        factor_of = factor_of * one(*cut)
    return factor_of


def scatter_about(own_key, shape, deviation, limit, shards=(), kind=jnp.bfloat16):
    array = jax.random.normal(own_key, shape, jnp.float32) * deviation
    if len(shards) > 0:
        array = block_levels(own_key, shape, shards, -0.22, 0.18) * array
    return jnp.clip(array, min=-limit, max=limit).astype(kind)


def noise_with(stream_key, extent, scale, most, split, heavy, kind=jnp.bfloat16):
    values = scale * jax.random.normal(stream_key, extent, jnp.float32)
    if split:
        values = values * block_levels(stream_key, extent, split, -0.22, 0.18)
    return jnp.clip(with_spikes(values, jax.random.fold_in(stream_key, 3), *heavy), -most, most).astype(kind)


def setup_inputs(seed: int = 0) -> dict:
    arg_keys = jax.random.split(jax.random.key(seed), 8)
    excitation = scatter_about(arg_keys[0], (STEPS, UNKNOWNS, EXC), 1.0, 6.0, ((1, 8), (2, 64)), jnp.float32)
    retarded = scatter_about(arg_keys[1], (DELAYS, UNKNOWNS, C), (C * DELAYS) ** -0.5, 0.0234375, ((0, 64), (1, 8)))
    history = noise_with(arg_keys[2], (DELAYS, UNKNOWNS, EXC), 1.0, 16.0, ((0, 64), (1, 8)), (0, 2, 64, 4.0))
    inverse = scatter_about(arg_keys[3], (UNKNOWNS, C), C ** -0.5, 0.25, ((0, 8),))
    transfer = scatter_about(arg_keys[4], (UNKNOWNS, 2 * M), (2 * M) ** -0.5, 0.375, ((0, 8),))
    faces = plant(jax.random.randint(arg_keys[5], (DOMAINS, 2 * M), 0, C), jax.random.fold_in(arg_keys[5], 1), 0, C - 1).astype(jnp.int32)
    counts = draw_counts(jax.random.fold_in(arg_keys[7], 71), 0)
    return {"excitation": excitation, "retarded": retarded, "history": history, "inverse": inverse, "transfer": transfer, "faces": faces, "counts": counts}


def reference(excitation, retarded, history, inverse, transfer, faces, counts):
    inverse_blocks = inverse.astype(jnp.float32).reshape(DOMAINS, C, C)
    transfer_blocks = transfer.astype(jnp.float32).reshape(DOMAINS, C, 2 * M)
    history_slots = history
    delay_ids = jnp.arange(DELAYS, dtype=jnp.int32)
    currents_list = []
    for step_index in range(STEPS):
        def add_delay(summed, delay_index):
            live_mask = (delay_index < counts).astype(jnp.float32)
            retarded_block = retarded[delay_index].astype(jnp.float32).reshape(DOMAINS, C, C)
            slot_data = history_slots[delay_index].astype(jnp.float32).reshape(DOMAINS, C, EXC)
            term = jnp.einsum("dab,dbn->dan", retarded_block, slot_data)
            return summed + live_mask[:, None, None] * term, None

        summed, unused = lax.scan(add_delay, jnp.zeros((DOMAINS, C, EXC), jnp.float32), delay_ids)
        right_side = (excitation[step_index].reshape(DOMAINS, C, EXC) - summed).astype(jnp.bfloat16)
        right_side = lax.optimization_barrier(right_side).astype(jnp.float32)
        first_pass = jnp.einsum("dab,dbn->dan", inverse_blocks, right_side)
        trace_rows = jnp.take_along_axis(first_pass, faces[:, :, None], axis=1).astype(jnp.bfloat16)
        trace_rows = lax.optimization_barrier(trace_rows).astype(jnp.float32)
        from_left = jnp.roll(trace_rows, 1, axis=0)[:, M:, :]
        from_right = jnp.roll(trace_rows, -1, axis=0)[:, :M, :]
        neighbour = jnp.concatenate([from_left, from_right], axis=1)
        coupling = jnp.einsum("dab,dbn->dan", transfer_blocks, neighbour).astype(jnp.bfloat16)
        coupling = lax.optimization_barrier(coupling).astype(jnp.float32)
        current = first_pass - jnp.einsum("dab,dbn->dan", inverse_blocks, coupling)
        current = current.reshape(UNKNOWNS, EXC)
        currents_list.append(current)
        history_slots = jnp.concatenate([current.astype(jnp.bfloat16)[None], history_slots[:-1]], axis=0)
    return jnp.stack(currents_list), history_slots
```

```python
import functools

import jax
import jax.numpy as jnp
from jax import lax
from jax.experimental import pallas as pl
from jax.experimental.pallas import tpu as pltpu
from jax.sharding import Mesh, PartitionSpec as P

Y, ZH, CORE, DOM = 8, 4, 2, 8
OWNERS = Y * CORE
DELAY = ("y", "zh", "c")
F32, BF16 = jnp.float32, jnp.bfloat16
VMEM = pl.BlockSpec(memory_space=pltpu.VMEM)
SMEM = pl.BlockSpec(memory_space=pltpu.SMEM)


def call(kernel, out_shape, in_specs, flops, nbytes, **more):
    out_specs = jax.tree.map(lambda _: VMEM, out_shape)
    return pl.pallas_call(
        kernel,
        out_shape=out_shape,
        in_specs=in_specs,
        out_specs=out_specs,
        compiler_params=pltpu.CompilerParams(vmem_limit_bytes=32 * 1024 * 1024),
        cost_estimate=pl.CostEstimate(flops=flops, bytes_accessed=nbytes, transcendentals=0),
        **more,
    )


def shape(dims, dtype):
    return jax.ShapeDtypeStruct(dims, dtype)


def dot(a, b):
    return jnp.dot(a, b, preferred_element_type=F32)


def dot_t(a, b):
    return lax.dot_general(a, b, (((1,), (1,)), ((), ())), preferred_element_type=F32)


def one_hot_rows(faces, rows):
    ids = lax.broadcasted_iota(jnp.int32, (rows, faces.shape[1]), 0)
    return (ids == faces).astype(F32).astype(BF16)


def position():
    return (lax.axis_index("y") * ZH + lax.axis_index("zh")) * CORE + lax.axis_index("c")


def live(counts, slot):
    return (position() * 2 + slot < counts[0]).astype(F32)


def own_partials(counts, exc, ret, hist, inv, faces, d0_ref, d1_ref, up_ref, down_ref, last_ref):
    last_ref[...] = hist[hist.shape[0] - 1]
    half = faces.shape[1] // 2
    rows = lax.broadcasted_iota(jnp.int32, (hist.shape[2], 1), 0)
    first_col = position() * 2
    m0, m1 = live(counts, 0), live(counts, 1)

    def placed(step):
        e = exc[step]
        return jnp.where(rows == first_col, e[0:1], jnp.where(rows == first_col + 1, e[1:2], 0.0))

    p0 = dot(ret[0], hist[0]) * m0 + dot(ret[1], hist[1]) * m1
    d0 = (placed(0) - p0.T).astype(BF16)
    d0_ref[...] = d0
    first = dot_t(d0, inv[...]).astype(BF16)
    trace = dot(first, one_hot_rows(faces[...], inv.shape[0])).astype(BF16)
    down_ref[...] = trace[:, :half]
    up_ref[...] = trace[:, half:]
    d1_ref[...] = placed(1) - (dot(ret[1], hist[0]) * m1).T


def pack_partials(counts, d0, d1, up, down, ret0, before, out):
    n = d0.shape[1]
    half = up.shape[1]
    out[:, :n] = d0[...]
    out[:, n : n + half] = up[...]
    out[:, n + half : n + 2 * half] = down[...]
    p1 = dot(ret0[...], before[...]) * live(counts, 0)
    out[:, n + 2 * half :] = (d1[...] - p1.T).astype(BF16)


def sum_and_copy(x, out):
    total = x[0].astype(F32)
    for i in range(1, x.shape[0]):
        total += x[i].astype(F32)
    total = total.astype(BF16)
    for i in range(out.shape[0]):
        out[i] = total


def two_firsts(counts, x, inv, tra, faces, r0_even, r0_odd, cur_ref, first_ref, up_ref, down_ref, r0, sem):
    odd = lax.axis_index("c") == 1

    @pl.when(odd)
    def _():
        copied(r0_odd, r0, sem)

    @pl.when(jnp.logical_not(odd))
    def _():
        copied(r0_even, r0, sem)

    n = inv.shape[0]
    faces_count = faces.shape[1]
    half = faces_count // 2
    total = x[0].astype(F32)
    for i in range(1, x.shape[0]):
        total += x[i].astype(F32)
    rhs = total[:, :n].astype(BF16)
    neighbour = total[:, n : n + faces_count].astype(BF16)
    d1 = total[:, n + faces_count :]
    coupling = dot_t(neighbour, tra[...]).astype(BF16)
    cur = dot_t(rhs, inv[...]) - dot_t(coupling, inv[...])
    cur_ref[...] = cur
    alive = (counts[0] > 0).astype(F32)
    newest = dot_t(cur.astype(BF16), r0[...]) * alive
    first = dot_t((d1 - newest).astype(BF16), inv[...])
    first_ref[...] = first
    trace = dot(first.astype(BF16), one_hot_rows(faces[...], n)).astype(BF16)
    down_ref[...] = trace[:, :half]
    up_ref[...] = trace[:, half:]


def second_current(cur0, first, up, down, inv, tra, gather_ref, share_ref):
    half = up.shape[1]
    coupling = dot_t(up[...], tra[:, :half]) + dot_t(down[...], tra[:, half:])
    cur1 = first[...] - dot_t(coupling.astype(BF16), inv[...])
    c0 = cur0[...]
    both = jnp.concatenate([cur1.astype(BF16), c0.astype(BF16)], axis=0)
    for i in range(gather_ref.shape[0]):
        gather_ref[i] = both
    for i in range(share_ref.shape[0]):
        q = 2 * (i % 4)
        share_ref[i, 0] = c0[q : q + 2]
        share_ref[i, 1] = cur1[q : q + 2]


def finish(gathered, shared, incoming, cur_ref, hist_ref, sem):
    source = lax.axis_index("zh") // 2
    cur_ref[...] = jnp.where(source == 0, shared[0], shared[1])
    leading = position() == 0

    @pl.when(leading)
    def _():
        owners, cols = gathered.shape[0], gathered.shape[1] // 2
        for slot in range(2):
            both = gathered[:, slot * cols : (slot + 1) * cols, :].reshape(owners * cols, -1)
            hist_ref[slot] = both.astype(F32).T.astype(BF16)

    @pl.when(jnp.logical_not(leading))
    def _():
        hist_ref[...] = incoming[...]


def copied(source, target, sem):
    copy = pltpu.make_async_copy(source, target, sem)
    copy.start()
    copy.wait()


def relay(held_at, first_at, held, first, second, after, out, sem):
    y = lax.axis_index("y")
    holds, from_first = one_of(y, held_at), one_of(y, first_at)

    @pl.when(holds)
    def _():
        copied(held, out, sem)

    @pl.when(jnp.logical_and(jnp.logical_not(holds), from_first))
    def _():
        copied(first, out, sem)

    @pl.when(jnp.logical_not(jnp.logical_or(holds, from_first)))
    def _():
        copied(second, out, sem)


def one_of(value, members):
    found = value == members[0]
    for member in members[1:]:
        found = jnp.logical_or(found, value == member)
    return found


def permute(value, axes, pairs):
    return lax.ppermute(value, axes, pairs)


def body(excitation, retarded, history, inverse, transfer, faces, counts):
    slots, n, width = history.shape
    steps = excitation.shape[0]
    half = faces.shape[1] // 2
    devices = Y * ZH * CORE
    cols = width // OWNERS
    exc = jnp.transpose(excitation, (0, 2, 1))
    any_spec = pl.BlockSpec(memory_space=pl.ANY)

    def at(yy, z, c):
        return (yy * ZH + z) * CORE + c

    def spread(value, *hops):
        return permute(value, DELAY, [(at(i, 0, 0), at(j, 0, 0)) for i, j in hops])

    def relayed(held_at, first_at, *operands):
        return call(
            functools.partial(relay, held_at, first_at),
            shape((n, n), BF16),
            [any_spec] * 4,
            0,
            1024 * 1024,
            scratch_shapes=[pltpu.SemaphoreType.DMA],
        )(*operands)

    ring = [(i, (i + 1) % DOM) for i in range(DOM)]
    back = [(j, i) for i, j in ring]
    chain = [(i, i + 1) for i in range(devices - 1)]

    r0 = retarded[0]
    s1a, s1b = spread(r0, (0, 3)), spread(r0, (0, 5))
    macs = n * n * width
    d0, d1, up, down, last = call(
        own_partials,
        (
            shape((width, n), BF16),
            shape((width, n), F32),
            shape((width, half), BF16),
            shape((width, half), BF16),
            shape((n, width), BF16),
        ),
        [SMEM] + [VMEM] * 5,
        2 * macs * 4,
        2 * 1024 * 1024,
    )(counts, exc, retarded, history, inverse, faces)
    up = permute(up, "dom", ring)
    down = permute(down, "dom", back)
    before = permute(last, DELAY, chain)
    lanes = 2 * n + 2 * half
    packed = call(pack_partials, shape((width, lanes), BF16), [SMEM] + [VMEM] * 6, 2 * macs, 1024 * 1024)(
        counts, d0, d1, up, down, r0, before
    )
    x = lax.all_to_all(packed.reshape(OWNERS, cols, lanes), ("y", "c"), 0, 0, tiled=True)
    r0 = relayed((0,), (3,), r0, s1a, s1b, packed)
    s2a, s2b = spread(r0, (0, 1), (3, 2), (5, 6)), spread(r0, (0, 7), (3, 4))
    x = call(sum_and_copy, shape((ZH, cols, lanes), BF16), [VMEM], 0, 512 * 1024)(x)
    r0 = relayed((0, 3, 5), (1, 2, 6), r0, s2a, s2b, x)
    x = lax.all_to_all(x, "zh", 0, 0, tiled=True)
    s3 = permute(r0, DELAY, [(at(i, 0, 0), at(i, 0, 1)) for i in range(Y)])

    cur0, first, up, down = call(
        two_firsts,
        (shape((cols, n), F32), shape((cols, n), F32), shape((cols, half), BF16), shape((cols, half), BF16)),
        [SMEM] + [VMEM] * 4 + [any_spec] * 2,
        2 * 8 * n * n * 6,
        2 * 1024 * 1024,
        scratch_shapes=[pltpu.VMEM((n, n), BF16), pltpu.SemaphoreType.DMA],
    )(counts, x, inverse, transfer, faces, r0, s3)
    up = permute(up, "dom", ring)
    down = permute(down, "dom", back)
    gather, share = call(
        second_current,
        (shape((OWNERS, 2 * cols, n), BF16), shape((ZH * CORE, steps, 2, n), F32)),
        [VMEM] * 6,
        2 * 8 * n * n * 2,
        1024 * 1024,
    )(cur0, first, up, down, inverse, transfer)
    incoming = permute(history, DELAY, chain)
    share = lax.all_to_all(share, ("zh", "c"), 0, 0, tiled=True)
    gather = lax.all_to_all(gather, ("y", "c"), 0, 0, tiled=True)
    share = lax.slice_in_dim(share, 0, 2, axis=0)
    currents, new_history = call(
        finish,
        (shape((steps, 2, n), F32), shape(history.shape, BF16)),
        [VMEM] * 3,
        0,
        1024 * 1024,
        scratch_shapes=[pltpu.SemaphoreType.DMA],
    )(gather, share, incoming)
    return jnp.transpose(currents, (0, 2, 1)), new_history


def solution(mesh):
    split = Mesh(mesh.devices.reshape(Y, ZH, CORE, DOM), ("y", "zh", "c", "dom"))
    placed = (
        P(None, "dom", DELAY),
        P(DELAY, "dom", None),
        P(DELAY, "dom", None),
        P("dom", None),
        P("dom", None),
        P("dom", None),
        P("dom"),
    )
    return jax.shard_map(
        body,
        mesh=split,
        in_specs=placed,
        out_specs=(P(None, "dom", DELAY), P(DELAY, "dom", None)),
        check_vma=False,
    )
```

```python
import functools

import jax
import jax.numpy as jnp
from jax import lax
from jax.experimental import pallas as pl
from jax.experimental.pallas import tpu as pltpu
from jax.sharding import Mesh, PartitionSpec as P

Y, ZH, CORE, DOM = 8, 4, 2, 8
OWNERS = Y * CORE
DELAY = ("y", "zh", "c")
F32, BF16 = jnp.float32, jnp.bfloat16
VMEM = pl.BlockSpec(memory_space=pltpu.VMEM)
SMEM = pl.BlockSpec(memory_space=pltpu.SMEM)
HBM = pl.BlockSpec(memory_space=pltpu.HBM)


def call(kernel, out_shape, in_specs, flops, nbytes, mib=32, out_specs=None, **more):
    if out_specs is None:
        out_specs = jax.tree.map(lambda _: VMEM, out_shape)
    return pl.pallas_call(
        kernel,
        out_shape=out_shape,
        in_specs=in_specs,
        out_specs=out_specs,
        compiler_params=pltpu.CompilerParams(vmem_limit_bytes=mib * 1024 * 1024),
        cost_estimate=pl.CostEstimate(flops=flops, bytes_accessed=nbytes, transcendentals=0),
        **more,
    )


def shape(dims, dtype):
    return jax.ShapeDtypeStruct(dims, dtype)


def dot(a, b):
    return jnp.dot(a, b, preferred_element_type=F32)


def dot_t(a, b):
    return lax.dot_general(a, b, (((1,), (1,)), ((), ())), preferred_element_type=F32)


def one_hot_rows(faces, rows):
    ids = lax.broadcasted_iota(jnp.int32, (rows, faces.shape[1]), 0)
    return (ids == faces).astype(F32).astype(BF16)


def position():
    return (lax.axis_index("y") * ZH + lax.axis_index("zh")) * CORE + lax.axis_index("c")


def live(counts, slot):
    return (position() * 2 + slot < counts[0]).astype(F32)


def copied(source, target, sem):
    copy = pltpu.make_async_copy(source, target, sem)
    copy.start()
    copy.wait()


def column_of(row):
    c, zh = (row // 8) % 2, (row // 2) % 4
    return (row // 16) * 16 + zh * 4 + c * 2 + row % 2


def permutation(width):
    cols = lax.broadcasted_iota(jnp.int32, (width, width), 0)
    rows = lax.broadcasted_iota(jnp.int32, (width, width), 1)
    return (cols == column_of(rows)).astype(F32).astype(BF16)


def permuted(block, order):
    return dot(block, order).astype(BF16)


def own_partials(
    counts, exc, faces, ret, hist, inv,
    d0_ref, d1_ref, up_ref, down_ref, r0_ref, h0_ref, h1_ref,
    r1, inv_v, exc_v, faces_v, sems,
):
    moves = [(hist.at[0], h0_ref), (ret.at[0], r0_ref), (hist.at[1], h1_ref), (ret.at[1], r1), (exc, exc_v)]
    moves += [(inv, inv_v), (faces, faces_v)]
    copies = [pltpu.make_async_copy(a, b, sems.at[k]) for k, (a, b) in enumerate(moves)]
    for copy in copies:
        copy.start()
    width = hist.shape[2]
    half = faces.shape[1] // 2
    col = column_of(lax.broadcasted_iota(jnp.int32, (width, 1), 0))
    first_col = position() * 2
    m0, m1 = live(counts, 0), live(counts, 1)
    order = permutation(width)

    def placed(step):
        e = exc_v[step]
        return jnp.where(col == first_col, e[0:1], jnp.where(col == first_col + 1, e[1:2], 0.0))

    copies[0].wait()
    h0 = permuted(h0_ref[...], order)
    copies[1].wait()
    p0 = dot(r0_ref[...], h0) * m0
    copies[2].wait()
    h1 = permuted(h1_ref[...], order)
    copies[3].wait()
    p0 += dot(r1[...], h1) * m1
    copies[4].wait()
    d0 = (placed(0) - p0.T).astype(BF16)
    d0_ref[...] = d0
    copies[5].wait()
    first = dot_t(d0, inv_v[...]).astype(BF16)
    copies[6].wait()
    trace = dot(first, one_hot_rows(faces_v[...], inv.shape[0])).astype(BF16)
    down_ref[...] = trace[:, :half]
    up_ref[...] = trace[:, half:]
    d1_ref[...] = placed(1) - (dot(r1[...], h0) * m1).T


def pack_partials(
    counts, d0, d1, up, down, r0, before, h0,
    out, h0_out, done_ref,
    d1_v, r0_v, before_v, p1_v, sems,
):
    n = d0.shape[1]
    half = up.shape[1]

    def place(start, length):
        return out.at[:, pl.ds(start, length)]

    moves = [(before, before_v), (r0, r0_v), (d1, d1_v)]
    moves += [(d0, place(0, n)), (up, place(n, half)), (down, place(n + half, half))]
    copies = [pltpu.make_async_copy(a, b, sems.at[k]) for k, (a, b) in enumerate(moves)]
    for copy in copies:
        copy.start()
    done_ref[...] = jnp.zeros_like(done_ref)
    order = permutation(before.shape[1])
    copies[0].wait()
    packed = permuted(before_v[...], order)
    copies[1].wait()
    p1 = dot(r0_v[...], packed) * live(counts, 0)
    copies[2].wait()
    p1_v[...] = (d1_v[...] - p1.T).astype(BF16)
    last = pltpu.make_async_copy(p1_v, place(n + 2 * half, n), sems.at[6])
    last.start()
    for copy in copies[3:]:
        copy.wait()
    last.wait()


def sum_and_copy(x, after, out):
    total = x[0].astype(F32)
    for i in range(1, x.shape[0]):
        total += x[i].astype(F32)
    total = total.astype(BF16)
    for i in range(out.shape[0]):
        out[i] = total


def two_firsts(counts, x, inv, tra, faces, r0_even, r0_odd, cur_ref, first_ref, up_ref, down_ref, r0, sem):
    odd = lax.axis_index("c") == 1

    @pl.when(odd)
    def _():
        copied(r0_odd, r0, sem)

    @pl.when(jnp.logical_not(odd))
    def _():
        copied(r0_even, r0, sem)

    n = inv.shape[0]
    faces_count = faces.shape[1]
    half = faces_count // 2
    total = x[0].astype(F32)
    for i in range(1, x.shape[0]):
        total += x[i].astype(F32)
    rhs = total[:, :n].astype(BF16)
    neighbour = total[:, n : n + faces_count].astype(BF16)
    d1 = total[:, n + faces_count :]
    coupling = dot_t(neighbour, tra[...]).astype(BF16)
    cur = dot_t(rhs, inv[...]) - dot_t(coupling, inv[...])
    cur_ref[...] = cur
    alive = (counts[0] > 0).astype(F32)
    newest = dot_t(cur.astype(BF16), r0[...]) * alive
    first = dot_t((d1 - newest).astype(BF16), inv[...])
    first_ref[...] = first
    trace = dot(first.astype(BF16), one_hot_rows(faces[...], n)).astype(BF16)
    down_ref[...] = trace[:, :half]
    up_ref[...] = trace[:, half:]


def second_current(cur0, first, up, down, inv, tra, gather_ref, *share_refs):
    half = up.shape[1]
    coupling = dot_t(up[...], tra[:, :half]) + dot_t(down[...], tra[:, half:])
    cur1 = first[...] - dot_t(coupling.astype(BF16), inv[...])
    c0 = cur0[...]
    both = jnp.concatenate([cur1.astype(BF16), c0.astype(BF16)], axis=0)
    for i in range(gather_ref.shape[0]):
        gather_ref[i] = both
    for i, share in enumerate(share_refs):
        share[0] = c0[2 * i : 2 * i + 2]
        share[1] = cur1[2 * i : 2 * i + 2]


def finish(gathered, s0, s1, s2, s3, before0, before1, cur_ref, hist_ref):
    zh = lax.axis_index("zh")
    cur_ref[...] = jnp.where(zh < 2, jnp.where(zh == 0, s0[...], s1[...]), jnp.where(zh == 2, s2[...], s3[...]))
    leading = position() == 0

    @pl.when(leading)
    def _():
        owners, cols = gathered.shape[0], gathered.shape[1] // 2
        order = permutation(owners * cols)
        for slot in range(2):
            both = gathered[:, slot * cols : (slot + 1) * cols, :].reshape(owners * cols, -1)
            hist_ref[slot] = dot_t(both.astype(F32).T.astype(BF16), order).astype(BF16)

    @pl.when(jnp.logical_not(leading))
    def _():
        hist_ref[0] = before0[...]
        hist_ref[1] = before1[...]


def relay(held_at, first_at, held, first, second, after, out, sem):
    y = lax.axis_index("y")
    holds, from_first = one_of(y, held_at), one_of(y, first_at)

    @pl.when(holds)
    def _():
        copied(held, out, sem)

    @pl.when(jnp.logical_and(jnp.logical_not(holds), from_first))
    def _():
        copied(first, out, sem)

    @pl.when(jnp.logical_not(jnp.logical_or(holds, from_first)))
    def _():
        copied(second, out, sem)


def one_of(value, members):
    found = value == members[0]
    for member in members[1:]:
        found = jnp.logical_or(found, value == member)
    return found


def permute(value, axes, pairs):
    return lax.ppermute(value, axes, pairs)


def body(excitation, retarded, history, inverse, transfer, faces, counts):
    slots, n, width = history.shape
    steps = excitation.shape[0]
    half = faces.shape[1] // 2
    devices = Y * ZH * CORE
    cols = width // OWNERS
    exc = jnp.transpose(excitation, (0, 2, 1))
    any_spec = pl.BlockSpec(memory_space=pl.ANY)

    def at(yy, z, c):
        return (yy * ZH + z) * CORE + c

    def spread(value, *hops):
        return permute(value, DELAY, [(at(i, 0, 0), at(j, 0, 0)) for i, j in hops])

    def relayed(held_at, first_at, *operands):
        return call(
            functools.partial(relay, held_at, first_at),
            shape((n, n), BF16),
            [any_spec] * 4,
            0,
            1024 * 1024,
            scratch_shapes=[pltpu.SemaphoreType.DMA],
        )(*operands)

    ring = [(i, (i + 1) % DOM) for i in range(DOM)]
    back = [(j, i) for i, j in ring]
    chain = [(i, i + 1) for i in range(devices - 1)]

    macs = n * n * width
    d0, d1, up, down, r0, h0, h1 = call(
        own_partials,
        (
            shape((width, n), BF16),
            shape((width, n), F32),
            shape((width, half), BF16),
            shape((width, half), BF16),
            shape((n, n), BF16),
            shape((n, width), BF16),
            shape((n, width), BF16),
        ),
        [SMEM] + [HBM] * 5,
        2 * macs * 4,
        2 * 1024 * 1024,
        mib=60,
        scratch_shapes=[
            pltpu.VMEM((n, n), BF16),
            pltpu.VMEM((n, n), BF16),
            pltpu.VMEM((steps, 2, n), F32),
            pltpu.VMEM(faces.shape, jnp.int32),
            pltpu.SemaphoreType.DMA((7,)),
        ],
    )(counts, exc, faces, retarded, history, inverse)
    up = permute(up, "dom", ring)
    down = permute(down, "dom", back)
    before = permute(h1, DELAY, chain)
    s1a, s1b = spread(r0, (0, 3)), spread(r0, (0, 5))
    lanes = 2 * n + 2 * half
    packed, h0, done = call(
        pack_partials,
        (shape((width, lanes), BF16), shape((n, width), BF16), shape((8, 128), F32)),
        [SMEM] + [any_spec] * 7,
        2 * macs,
        1024 * 1024,
        mib=60,
        out_specs=(any_spec, any_spec, VMEM),
        input_output_aliases={7: 1},
        scratch_shapes=[
            pltpu.VMEM((width, n), F32),
            pltpu.VMEM((n, n), BF16),
            pltpu.VMEM((n, width), BF16),
            pltpu.VMEM((width, n), BF16),
            pltpu.SemaphoreType.DMA((7,)),
        ],
    )(counts, d0, d1, up, down, r0, before, h0)
    x = lax.all_to_all(packed.reshape(OWNERS, cols, lanes), ("y", "c"), 0, 0, tiled=True)
    before0 = permute(h0, DELAY, chain)
    r0 = relayed((0,), (3,), r0, s1a, s1b, done)
    s2a, s2b = spread(r0, (0, 1), (3, 2), (5, 6)), spread(r0, (0, 7), (3, 4))
    x = call(sum_and_copy, shape((ZH, cols, lanes), BF16), [VMEM, any_spec], 0, 512 * 1024)(x, before0)
    r0 = relayed((0, 3, 5), (1, 2, 6), r0, s2a, s2b, x)
    x = lax.all_to_all(x, "zh", 0, 0, tiled=True)
    s3 = permute(r0, DELAY, [(at(i, 0, 0), at(i, 0, 1)) for i in range(Y)])

    cur0, first, up, down = call(
        two_firsts,
        (shape((cols, n), F32), shape((cols, n), F32), shape((cols, half), BF16), shape((cols, half), BF16)),
        [SMEM] + [VMEM] * 4 + [any_spec] * 2,
        2 * 8 * n * n * 6,
        2 * 1024 * 1024,
        scratch_shapes=[pltpu.VMEM((n, n), BF16), pltpu.SemaphoreType.DMA],
    )(counts, x, inverse, transfer, faces, r0, s3)
    up = permute(up, "dom", ring)
    down = permute(down, "dom", back)
    gather, *share = call(
        second_current,
        [shape((OWNERS, 2 * cols, n), BF16)] + [shape((steps, 2, n), F32)] * ZH,
        [VMEM] * 6,
        2 * 8 * n * n * 2,
        1024 * 1024,
    )(cur0, first, up, down, inverse, transfer)
    gather = lax.all_to_all(gather, ("y", "c"), 0, 0, tiled=True)
    for z in range(1, ZH):
        share[z] = permute(share[z], DELAY, [(at(i, 0, c), at(i, z, c)) for i in range(Y) for c in range(CORE)])
    currents, new_history = call(
        finish,
        (shape((steps, 2, n), F32), shape(history.shape, BF16)),
        [VMEM] * 7,
        0,
        1024 * 1024,
    )(gather, *share, before0, before)
    return jnp.transpose(currents, (0, 2, 1)), new_history


def solution(mesh):
    split = Mesh(mesh.devices.reshape(Y, ZH, CORE, DOM), ("y", "zh", "c", "dom"))
    placed = (
        P(None, "dom", DELAY),
        P(DELAY, "dom", None),
        P(DELAY, "dom", None),
        P("dom", None),
        P("dom", None),
        P("dom", None),
        P("dom"),
    )
    return jax.shard_map(
        body,
        mesh=split,
        in_specs=placed,
        out_specs=(P(None, "dom", DELAY), P(DELAY, "dom", None)),
        check_vma=False,
    )
```

```python
import functools

import jax
import jax.numpy as jnp
from jax import lax
from jax.experimental import pallas as pl
from jax.experimental.pallas import tpu as pltpu
from jax.sharding import Mesh, PartitionSpec as P

Y, ZH, CORE, DOM = 8, 4, 2, 8
OWNERS = Y * CORE
DELAY = ("y", "zh", "c")
F32, BF16 = jnp.float32, jnp.bfloat16
VMEM = pl.BlockSpec(memory_space=pltpu.VMEM)
SMEM = pl.BlockSpec(memory_space=pltpu.SMEM)


def call(kernel, out_shape, in_specs, flops, nbytes, mib=32, out_specs=None, **more):
    if out_specs is None:
        out_specs = jax.tree.map(lambda _: VMEM, out_shape)
    return pl.pallas_call(
        kernel,
        out_shape=out_shape,
        in_specs=in_specs,
        out_specs=out_specs,
        compiler_params=pltpu.CompilerParams(vmem_limit_bytes=mib * 1024 * 1024),
        cost_estimate=pl.CostEstimate(flops=flops, bytes_accessed=nbytes, transcendentals=0),
        **more,
    )


def shape(dims, dtype):
    return jax.ShapeDtypeStruct(dims, dtype)


def dot(a, b):
    return jnp.dot(a, b, preferred_element_type=F32)


def dot_t(a, b):
    return lax.dot_general(a, b, (((1,), (1,)), ((), ())), preferred_element_type=F32)


def one_hot_rows(faces, rows):
    ids = lax.broadcasted_iota(jnp.int32, (rows, faces.shape[1]), 0)
    return (ids == faces).astype(F32).astype(BF16)


def position():
    return (lax.axis_index("y") * ZH + lax.axis_index("zh")) * CORE + lax.axis_index("c")


def live(counts, slot):
    return (position() * 2 + slot < counts[0]).astype(F32)


def copied(source, target, sem):
    copy = pltpu.make_async_copy(source, target, sem)
    copy.start()
    copy.wait()


def column_of(row):
    c, zh = (row // 8) % 2, (row // 2) % 4
    return (row // 16) * 16 + zh * 4 + c * 2 + row % 2


def permutation(width):
    cols = lax.broadcasted_iota(jnp.int32, (width, width), 0)
    rows = lax.broadcasted_iota(jnp.int32, (width, width), 1)
    return (cols == column_of(rows)).astype(F32).astype(BF16)


def permuted(block, order):
    return dot(block, order).astype(BF16)


def selections(faces, select_ref, order_ref):
    select_ref[...] = one_hot_rows(faces[...], select_ref.shape[0])
    order_ref[...] = permutation(order_ref.shape[0])


def own_partials(
    counts, exc, select, order, hist, ret, inv,
    d0_ref, d1_ref, up_ref, down_ref, r0_ref,
    r1, inv_v, sems,
):
    moves = [(ret.at[0], r0_ref), (ret.at[1], r1), (inv, inv_v)]
    copies = [pltpu.make_async_copy(a, b, sems.at[k]) for k, (a, b) in enumerate(moves)]
    for copy in copies:
        copy.start()
    width = hist.shape[2]
    half = select.shape[1] // 2
    col = column_of(lax.broadcasted_iota(jnp.int32, (width, 1), 0))
    first_col = position() * 2
    m0, m1 = live(counts, 0), live(counts, 1)

    def placed(step):
        e = exc[step]
        return jnp.where(col == first_col, e[0:1], jnp.where(col == first_col + 1, e[1:2], 0.0))

    h0, h1 = permuted(hist[0], order[...]), permuted(hist[1], order[...])
    copies[0].wait()
    p0 = dot(r0_ref[...], h0) * m0
    copies[1].wait()
    p0 += dot(r1[...], h1) * m1
    d0 = (placed(0) - p0.T).astype(BF16)
    d0_ref[...] = d0
    copies[2].wait()
    first = dot_t(d0, inv_v[...]).astype(BF16)
    trace = dot(first, select[...]).astype(BF16)
    down_ref[...] = trace[:, :half]
    up_ref[...] = trace[:, half:]
    d1_ref[...] = placed(1) - (dot(r1[...], h0) * m1).T


def pack_partials(counts, order, d0, d1, up, down, r0, before, out):
    n = d0.shape[1]
    half = up.shape[1]
    out[:, :n] = d0[...]
    out[:, n : n + half] = up[...]
    out[:, n + half : n + 2 * half] = down[...]
    p1 = dot(r0[...], permuted(before[1], order[...])) * live(counts, 0)
    out[:, n + 2 * half :] = (d1[...] - p1.T).astype(BF16)


def sum_parts(x, out):
    total = x[0].astype(F32)
    for i in range(1, x.shape[0]):
        total += x[i].astype(F32)
    out[...] = total


def two_firsts(counts, x0, x1, x2, x3, inv, tra, select, r0_even, r0_odd, cur_ref, first_ref, up_ref, down_ref, r0, sem):
    odd = lax.axis_index("c") == 1

    @pl.when(odd)
    def _():
        copied(r0_odd, r0, sem)

    @pl.when(jnp.logical_not(odd))
    def _():
        copied(r0_even, r0, sem)

    n = inv.shape[0]
    faces_count = select.shape[1]
    half = faces_count // 2
    total = (x0[...] + x1[...]) + (x2[...] + x3[...])
    rhs = total[:, :n].astype(BF16)
    neighbour = total[:, n : n + faces_count].astype(BF16)
    d1 = total[:, n + faces_count :]
    coupling = dot_t(neighbour, tra[...]).astype(BF16)
    cur = dot_t(rhs, inv[...]) - dot_t(coupling, inv[...])
    cur_ref[...] = cur
    alive = (counts[0] > 0).astype(F32)
    newest = dot_t(cur.astype(BF16), r0[...]) * alive
    first = dot_t((d1 - newest).astype(BF16), inv[...])
    first_ref[...] = first
    trace = dot(first.astype(BF16), select[...]).astype(BF16)
    down_ref[...] = trace[:, :half]
    up_ref[...] = trace[:, half:]


def second_current(cur0, first, up, down, inv, tra, gather_ref, *share_refs):
    half = up.shape[1]
    coupling = dot_t(up[...], tra[:, :half]) + dot_t(down[...], tra[:, half:])
    cur1 = first[...] - dot_t(coupling.astype(BF16), inv[...])
    c0 = cur0[...]
    both = jnp.concatenate([cur1.astype(BF16), c0.astype(BF16)], axis=0)
    for i in range(gather_ref.shape[0]):
        gather_ref[i] = both
    for i, share in enumerate(share_refs):
        share[0] = c0[2 * i : 2 * i + 2]
        share[1] = cur1[2 * i : 2 * i + 2]


def finish(gathered, s0, s1, s2, s3, before, cur_ref, hist_ref):
    zh = lax.axis_index("zh")
    cur_ref[...] = jnp.where(zh < 2, jnp.where(zh == 0, s0[...], s1[...]), jnp.where(zh == 2, s2[...], s3[...]))
    leading = position() == 0

    @pl.when(leading)
    def _():
        owners, cols = gathered.shape[0], gathered.shape[1] // 2
        order = permutation(owners * cols)
        for slot in range(2):
            both = gathered[:, slot * cols : (slot + 1) * cols, :].reshape(owners * cols, -1)
            hist_ref[slot] = dot_t(both.astype(F32).T.astype(BF16), order).astype(BF16)

    @pl.when(jnp.logical_not(leading))
    def _():
        hist_ref[...] = before[...]


def relay(held_at, first_at, held, first, second, after, out, sem):
    y = lax.axis_index("y")
    holds, from_first = one_of(y, held_at), one_of(y, first_at)

    @pl.when(holds)
    def _():
        copied(held, out, sem)

    @pl.when(jnp.logical_and(jnp.logical_not(holds), from_first))
    def _():
        copied(first, out, sem)

    @pl.when(jnp.logical_not(jnp.logical_or(holds, from_first)))
    def _():
        copied(second, out, sem)


def one_of(value, members):
    found = value == members[0]
    for member in members[1:]:
        found = jnp.logical_or(found, value == member)
    return found


def permute(value, axes, pairs):
    return lax.ppermute(value, axes, pairs)


def body(excitation, retarded, history, inverse, transfer, faces, counts):
    slots, n, width = history.shape
    steps = excitation.shape[0]
    half = faces.shape[1] // 2
    devices = Y * ZH * CORE
    cols = width // OWNERS
    exc = jnp.transpose(excitation, (0, 2, 1))
    any_spec = pl.BlockSpec(memory_space=pl.ANY)

    def at(yy, z, c):
        return (yy * ZH + z) * CORE + c

    def spread(value, *hops):
        return permute(value, DELAY, [(at(i, 0, 0), at(j, 0, 0)) for i, j in hops])

    def relayed(held_at, first_at, *operands):
        return call(
            functools.partial(relay, held_at, first_at),
            shape((n, n), BF16),
            [any_spec] * 4,
            0,
            1024 * 1024,
            scratch_shapes=[pltpu.SemaphoreType.DMA],
        )(*operands)

    ring = [(i, (i + 1) % DOM) for i in range(DOM)]
    back = [(j, i) for i, j in ring]
    chain = [(i, i + 1) for i in range(devices - 1)]

    macs = n * n * width
    before = permute(history, DELAY, chain)
    select, order = call(
        selections,
        (shape((n, 2 * half), BF16), shape((width, width), BF16)),
        [VMEM],
        64 * 1024 * 1024,
        8 * 1024 * 1024,
    )(faces)
    d0, d1, up, down, r0 = call(
        own_partials,
        (
            shape((width, n), BF16),
            shape((width, n), F32),
            shape((width, half), BF16),
            shape((width, half), BF16),
            shape((n, n), BF16),
        ),
        [SMEM] + [VMEM] * 4 + [any_spec] * 2,
        2 * macs * 4,
        2 * 1024 * 1024,
        mib=52,
        scratch_shapes=[pltpu.VMEM((n, n), BF16), pltpu.VMEM((n, n), BF16), pltpu.SemaphoreType.DMA((3,))],
    )(counts, exc, select, order, history, retarded, inverse)
    up = permute(up, "dom", ring)
    down = permute(down, "dom", back)
    s1a, s1b = spread(r0, (0, 3)), spread(r0, (0, 5))
    lanes = 2 * n + 2 * half
    packed = call(pack_partials, shape((width, lanes), BF16), [SMEM] + [VMEM] * 7, 2 * macs, 1024 * 1024)(
        counts, order, d0, d1, up, down, r0, before
    )
    x = lax.all_to_all(packed.reshape(OWNERS, cols, lanes), ("y", "c"), 0, 0, tiled=True)
    r0 = relayed((0,), (3,), r0, s1a, s1b, packed)
    s2a, s2b = spread(r0, (0, 1), (3, 2), (5, 6)), spread(r0, (0, 7), (3, 4))
    x = call(sum_parts, shape((cols, lanes), F32), [VMEM], 0, 512 * 1024)(x)
    xs = [x] + [permute(x, "zh", [(z, 0)]) for z in range(1, ZH)]
    r0 = relayed((0, 3, 5), (1, 2, 6), r0, s2a, s2b, x)
    s3 = permute(r0, DELAY, [(at(i, 0, 0), at(i, 0, 1)) for i in range(Y)])

    cur0, first, up, down = call(
        two_firsts,
        (shape((cols, n), F32), shape((cols, n), F32), shape((cols, half), BF16), shape((cols, half), BF16)),
        [SMEM] + [VMEM] * 7 + [any_spec] * 2,
        2 * 8 * n * n * 6,
        2 * 1024 * 1024,
        scratch_shapes=[pltpu.VMEM((n, n), BF16), pltpu.SemaphoreType.DMA],
    )(counts, *xs, inverse, transfer, select, r0, s3)
    up = permute(up, ("zh", "dom"), ring)
    down = permute(down, ("zh", "dom"), back)
    gather, *share = call(
        second_current,
        [shape((OWNERS, 2 * cols, n), BF16)] + [shape((steps, 2, n), F32)] * ZH,
        [VMEM] * 6,
        2 * 8 * n * n * 2,
        1024 * 1024,
    )(cur0, first, up, down, inverse, transfer)
    gather = lax.all_to_all(gather, ("y", "c"), 0, 0, tiled=True)
    for z in range(1, ZH):
        share[z] = permute(share[z], DELAY, [(at(i, 0, c), at(i, z, c)) for i in range(Y) for c in range(CORE)])
    currents, new_history = call(
        finish,
        (shape((steps, 2, n), F32), shape(history.shape, BF16)),
        [VMEM] * 6,
        0,
        1024 * 1024,
    )(gather, *share, before)
    return jnp.transpose(currents, (0, 2, 1)), new_history


def solution(mesh):
    split = Mesh(mesh.devices.reshape(Y, ZH, CORE, DOM), ("y", "zh", "c", "dom"))
    placed = (
        P(None, "dom", DELAY),
        P(DELAY, "dom", None),
        P(DELAY, "dom", None),
        P("dom", None),
        P("dom", None),
        P("dom", None),
        P("dom"),
    )
    return jax.shard_map(
        body,
        mesh=split,
        in_specs=placed,
        out_specs=(P(None, "dom", DELAY), P(DELAY, "dom", None)),
        check_vma=False,
    )
```

```python
import functools

import jax
import jax.numpy as jnp
from jax import lax
from jax.experimental import pallas as pl
from jax.experimental.pallas import tpu as pltpu
from jax.sharding import Mesh, PartitionSpec as P

Y, ZH, CORE, DOM = 8, 4, 2, 8
OWNERS = Y * CORE
DELAY = ("y", "zh", "c")
F32, BF16 = jnp.float32, jnp.bfloat16
VMEM = pl.BlockSpec(memory_space=pltpu.VMEM)
SMEM = pl.BlockSpec(memory_space=pltpu.SMEM)


def call(kernel, out_shape, in_specs, flops, nbytes, mib=32, out_specs=None, **more):
    if out_specs is None:
        out_specs = jax.tree.map(lambda _: VMEM, out_shape)
    return pl.pallas_call(
        kernel,
        out_shape=out_shape,
        in_specs=in_specs,
        out_specs=out_specs,
        compiler_params=pltpu.CompilerParams(vmem_limit_bytes=mib * 1024 * 1024),
        cost_estimate=pl.CostEstimate(flops=flops, bytes_accessed=nbytes, transcendentals=0),
        **more,
    )


def shape(dims, dtype):
    return jax.ShapeDtypeStruct(dims, dtype)


def dot(a, b):
    return jnp.dot(a, b, preferred_element_type=F32)


def dot_t(a, b):
    return lax.dot_general(a, b, (((1,), (1,)), ((), ())), preferred_element_type=F32)


def one_hot_rows(faces, rows):
    ids = lax.broadcasted_iota(jnp.int32, (rows, faces.shape[1]), 0)
    return (ids == faces).astype(F32).astype(BF16)


def position():
    return (lax.axis_index("y") * ZH + lax.axis_index("zh")) * CORE + lax.axis_index("c")


def live(counts, slot):
    return (position() * 2 + slot < counts[0]).astype(F32)


def copied(source, target, sem):
    copy = pltpu.make_async_copy(source, target, sem)
    copy.start()
    copy.wait()


def column_of(row):
    c, zh = (row // 8) % 2, (row // 2) % 4
    return (row // 16) * 16 + zh * 4 + c * 2 + row % 2


def permutation(width):
    cols = lax.broadcasted_iota(jnp.int32, (width, width), 0)
    rows = lax.broadcasted_iota(jnp.int32, (width, width), 1)
    return (cols == column_of(rows)).astype(F32).astype(BF16)


def permuted(block, order):
    return dot(block, order).astype(BF16)


def selections(faces, ret, select_ref, order_ref, r0_ref, sem):
    copy = pltpu.make_async_copy(ret.at[0], r0_ref, sem)
    copy.start()
    select_ref[...] = one_hot_rows(faces[...], select_ref.shape[0])
    order_ref[...] = permutation(order_ref.shape[0])
    copy.wait()


def own_partials(counts, exc, order, hist, r0, ret, d0_ref, d1_ref, r1, sem):
    copy = pltpu.make_async_copy(ret.at[1], r1, sem)
    copy.start()
    width = hist.shape[2]
    col = column_of(lax.broadcasted_iota(jnp.int32, (width, 1), 0))
    first_col = position() * 2
    m0, m1 = live(counts, 0), live(counts, 1)

    def placed(step):
        e = exc[step]
        return jnp.where(col == first_col, e[0:1], jnp.where(col == first_col + 1, e[1:2], 0.0))

    h0, h1 = permuted(hist[0], order[...]), permuted(hist[1], order[...])
    p0 = dot(r0[...], h0) * m0
    copy.wait()
    p0 += dot(r1[...], h1) * m1
    d0_ref[...] = (placed(0) - p0.T).astype(BF16)
    d1_ref[...] = placed(1) - (dot(r1[...], h0) * m1).T


def pack_partials(counts, order, d0, d1, r0, before, out):
    n = d0.shape[1]
    out[:, :n] = d0[...]
    p1 = dot(r0[...], permuted(before[1], order[...])) * live(counts, 0)
    out[:, n:] = (d1[...] - p1.T).astype(BF16)


def sum_parts(x, out):
    total = x[0].astype(F32)
    for i in range(1, x.shape[0]):
        total += x[i].astype(F32)
    out[...] = total


def trace_of(first, select, up_ref, down_ref):
    trace = dot(first.astype(BF16), select[...]).astype(BF16)
    half = select.shape[1] // 2
    down_ref[...] = trace[:, :half]
    up_ref[...] = trace[:, half:]


def coupled(up, down, inv, tra):
    half = up.shape[1]
    coupling = dot_t(up[...], tra[:, :half]) + dot_t(down[...], tra[:, half:])
    return dot_t(coupling.astype(BF16), inv[...])


def first_of_sum(x0, x1, x2, x3, inv, select, first_ref, rest_ref, up_ref, down_ref):
    n = inv.shape[0]
    total = (x0[...] + x1[...]) + (x2[...] + x3[...])
    first = dot_t(total[:, :n].astype(BF16), inv[...])
    first_ref[...] = first
    rest_ref[...] = total[:, n:]
    trace_of(first, select, up_ref, down_ref)


def next_first(
    counts, first, rest, up, down, inv, tra, select, r0_even, r0_odd,
    cur_ref, first_ref, up_ref, down_ref,
    r0, sem,
):
    odd = lax.axis_index("c") == 1

    @pl.when(odd)
    def _():
        copied(r0_odd, r0, sem)

    @pl.when(jnp.logical_not(odd))
    def _():
        copied(r0_even, r0, sem)

    cur = first[...] - coupled(up, down, inv, tra)
    cur_ref[...] = cur
    alive = (counts[0] > 0).astype(F32)
    newest = dot_t(cur.astype(BF16), r0[...]) * alive
    following = dot_t((rest[...] - newest).astype(BF16), inv[...])
    first_ref[...] = following
    trace_of(following, select, up_ref, down_ref)


def second_current(cur0, first, up, down, inv, tra, gather_ref, *share_refs):
    cur1 = first[...] - coupled(up, down, inv, tra)
    c0 = cur0[...]
    both = jnp.concatenate([cur1.astype(BF16), c0.astype(BF16)], axis=0)
    for i in range(gather_ref.shape[0]):
        gather_ref[i] = both
    for i, share in enumerate(share_refs):
        share[0] = c0[2 * i : 2 * i + 2]
        share[1] = cur1[2 * i : 2 * i + 2]


def finish(gathered, s0, s1, s2, s3, before, cur_ref, hist_ref):
    zh = lax.axis_index("zh")
    cur_ref[...] = jnp.where(zh < 2, jnp.where(zh == 0, s0[...], s1[...]), jnp.where(zh == 2, s2[...], s3[...]))
    leading = position() == 0

    @pl.when(leading)
    def _():
        owners, cols = gathered.shape[0], gathered.shape[1] // 2
        order = permutation(owners * cols)
        for slot in range(2):
            both = gathered[:, slot * cols : (slot + 1) * cols, :].reshape(owners * cols, -1)
            hist_ref[slot] = dot_t(both.astype(F32).T.astype(BF16), order).astype(BF16)

    @pl.when(jnp.logical_not(leading))
    def _():
        hist_ref[...] = before[...]


def relay(held_at, first_at, held, first, second, after, out, sem):
    y = lax.axis_index("y")
    holds, from_first = one_of(y, held_at), one_of(y, first_at)

    @pl.when(holds)
    def _():
        copied(held, out, sem)

    @pl.when(jnp.logical_and(jnp.logical_not(holds), from_first))
    def _():
        copied(first, out, sem)

    @pl.when(jnp.logical_not(jnp.logical_or(holds, from_first)))
    def _():
        copied(second, out, sem)


def one_of(value, members):
    found = value == members[0]
    for member in members[1:]:
        found = jnp.logical_or(found, value == member)
    return found


def permute(value, axes, pairs):
    return lax.ppermute(value, axes, pairs)


def body(excitation, retarded, history, inverse, transfer, faces, counts):
    slots, n, width = history.shape
    steps = excitation.shape[0]
    half = faces.shape[1] // 2
    devices = Y * ZH * CORE
    cols = width // OWNERS
    exc = jnp.transpose(excitation, (0, 2, 1))
    any_spec = pl.BlockSpec(memory_space=pl.ANY)

    def at(yy, z, c):
        return (yy * ZH + z) * CORE + c

    def spread(value, *hops):
        return permute(value, DELAY, [(at(i, 0, 0), at(j, 0, 0)) for i, j in hops])

    def relayed(held_at, first_at, *operands):
        return call(
            functools.partial(relay, held_at, first_at),
            shape((n, n), BF16),
            [any_spec] * 4,
            0,
            1024 * 1024,
            scratch_shapes=[pltpu.SemaphoreType.DMA],
        )(*operands)

    ring = [(i, (i + 1) % DOM) for i in range(DOM)]
    back = [(j, i) for i, j in ring]
    chain = [(i, i + 1) for i in range(devices - 1)]

    macs = n * n * width
    before = permute(history, DELAY, chain)
    select, order, r0 = call(
        selections,
        (shape((n, 2 * half), BF16), shape((width, width), BF16), shape((n, n), BF16)),
        [VMEM, any_spec],
        0,
        1024 * 1024,
        mib=53,
        scratch_shapes=[pltpu.SemaphoreType.DMA],
    )(faces, retarded)
    d0, d1 = call(
        own_partials,
        (shape((width, n), BF16), shape((width, n), F32)),
        [SMEM] + [VMEM] * 4 + [any_spec],
        2 * macs * 4,
        2 * 1024 * 1024,
        mib=52,
        scratch_shapes=[pltpu.VMEM((n, n), BF16), pltpu.SemaphoreType.DMA],
    )(counts, exc, order, history, r0, retarded)
    s1a, s1b = spread(r0, (0, 3)), spread(r0, (0, 5))
    lanes = 2 * n
    packed = call(pack_partials, shape((width, lanes), BF16), [SMEM] + [VMEM] * 5, 2 * macs, 1024 * 1024)(
        counts, order, d0, d1, r0, before
    )
    x = lax.all_to_all(packed.reshape(OWNERS, cols, lanes), ("y", "c"), 0, 0, tiled=True)
    r0 = relayed((0,), (3,), r0, s1a, s1b, packed)
    s2a, s2b = spread(r0, (0, 1), (3, 2), (5, 6)), spread(r0, (0, 7), (3, 4))
    x = call(sum_parts, shape((cols, lanes), F32), [VMEM], 0, 512 * 1024)(x)
    xs = [x] + [permute(x, "zh", [(z, 0)]) for z in range(1, ZH)]
    r0 = relayed((0, 3, 5), (1, 2, 6), r0, s2a, s2b, xs[1])
    s3 = permute(r0, DELAY, [(at(i, 0, 0), at(i, 0, 1)) for i in range(Y)])

    def halo(up, down):
        return permute(up, ("zh", "dom"), ring), permute(down, ("zh", "dom"), back)

    trace_shape = (shape((cols, half), BF16),) * 2
    first, rest, up, down = call(
        first_of_sum,
        (shape((cols, n), F32), shape((cols, n), F32)) + trace_shape,
        [VMEM] * 6,
        2 * 8 * n * n * 2,
        1024 * 1024,
    )(*xs, inverse, select)
    up, down = halo(up, down)
    cur0, first, up, down = call(
        next_first,
        (shape((cols, n), F32), shape((cols, n), F32)) + trace_shape,
        [SMEM] + [VMEM] * 7 + [any_spec] * 2,
        2 * 8 * n * n * 5,
        2 * 1024 * 1024,
        scratch_shapes=[pltpu.VMEM((n, n), BF16), pltpu.SemaphoreType.DMA],
    )(counts, first, rest, up, down, inverse, transfer, select, r0, s3)
    up, down = halo(up, down)
    gather, *share = call(
        second_current,
        [shape((OWNERS, 2 * cols, n), BF16)] + [shape((steps, 2, n), F32)] * ZH,
        [VMEM] * 6,
        2 * 8 * n * n * 2,
        1024 * 1024,
    )(cur0, first, up, down, inverse, transfer)
    gather = lax.all_to_all(gather, ("y", "c"), 0, 0, tiled=True)
    for z in range(1, ZH):
        share[z] = permute(share[z], DELAY, [(at(i, 0, c), at(i, z, c)) for i in range(Y) for c in range(CORE)])
    currents, new_history = call(
        finish,
        (shape((steps, 2, n), F32), shape(history.shape, BF16)),
        [VMEM] * 6,
        0,
        1024 * 1024,
    )(gather, *share, before)
    return jnp.transpose(currents, (0, 2, 1)), new_history


def solution(mesh):
    split = Mesh(mesh.devices.reshape(Y, ZH, CORE, DOM), ("y", "zh", "c", "dom"))
    placed = (
        P(None, "dom", DELAY),
        P(DELAY, "dom", None),
        P(DELAY, "dom", None),
        P("dom", None),
        P("dom", None),
        P("dom", None),
        P("dom"),
    )
    return jax.shard_map(
        body,
        mesh=split,
        in_specs=placed,
        out_specs=(P(None, "dom", DELAY), P(DELAY, "dom", None)),
        check_vma=False,
    )
```

```python
import functools

import jax
import jax.numpy as jnp
from jax import lax
from jax.experimental import pallas as pl
from jax.experimental.pallas import tpu as pltpu
from jax.sharding import Mesh, PartitionSpec as P

Y, ZH, CORE, DOM = 8, 4, 2, 8
OWNERS = Y * CORE
DELAY = ("y", "zh", "c")
F32, BF16 = jnp.float32, jnp.bfloat16
VMEM = pl.BlockSpec(memory_space=pltpu.VMEM)
SMEM = pl.BlockSpec(memory_space=pltpu.SMEM)


def call(kernel, out_shape, in_specs, flops, nbytes, mib=32, out_specs=None, **more):
    if out_specs is None:
        out_specs = jax.tree.map(lambda _: VMEM, out_shape)
    return pl.pallas_call(
        kernel,
        out_shape=out_shape,
        in_specs=in_specs,
        out_specs=out_specs,
        compiler_params=pltpu.CompilerParams(vmem_limit_bytes=mib * 1024 * 1024),
        cost_estimate=pl.CostEstimate(flops=flops, bytes_accessed=nbytes, transcendentals=0),
        **more,
    )


def shape(dims, dtype):
    return jax.ShapeDtypeStruct(dims, dtype)


def dot(a, b):
    return jnp.dot(a, b, preferred_element_type=F32)


def dot_t(a, b):
    return lax.dot_general(a, b, (((1,), (1,)), ((), ())), preferred_element_type=F32)


def one_hot_rows(faces, rows):
    ids = lax.broadcasted_iota(jnp.int32, (rows, faces.shape[1]), 0)
    return (ids == faces).astype(F32).astype(BF16)


def position():
    return (lax.axis_index("y") * ZH + lax.axis_index("zh")) * CORE + lax.axis_index("c")


def live(counts, slot):
    return (position() * 2 + slot < counts[0]).astype(F32)


def copied(source, target, sem):
    copy = pltpu.make_async_copy(source, target, sem)
    copy.start()
    copy.wait()


def column_of(row):
    c, zh = (row // 8) % 2, (row // 2) % 4
    return (row // 16) * 16 + zh * 4 + c * 2 + row % 2


def permutation(width):
    cols = lax.broadcasted_iota(jnp.int32, (width, width), 0)
    rows = lax.broadcasted_iota(jnp.int32, (width, width), 1)
    return (cols == column_of(rows)).astype(F32).astype(BF16)


def permuted(block, order):
    return dot(block, order).astype(BF16)


def selections(faces, ret, hist, select_ref, order_ref, r0_ref, h1_ref, sems):
    moves = [(hist.at[hist.shape[0] - 1], h1_ref), (ret.at[0], r0_ref)]
    copies = [pltpu.make_async_copy(a, b, sems.at[k]) for k, (a, b) in enumerate(moves)]
    for copy in copies:
        copy.start()
    select_ref[...] = one_hot_rows(faces[...], select_ref.shape[0])
    order_ref[...] = permutation(order_ref.shape[0])
    for copy in copies:
        copy.wait()


def own_partials(
    counts, exc, select, order, hist, r0, ret, inv,
    d0_ref, d1_ref, up_ref, down_ref,
    r1, inv_v, sems,
):
    moves = [(ret.at[1], r1), (inv, inv_v)]
    copies = [pltpu.make_async_copy(a, b, sems.at[k]) for k, (a, b) in enumerate(moves)]
    for copy in copies:
        copy.start()
    width = hist.shape[2]
    half = select.shape[1] // 2
    col = column_of(lax.broadcasted_iota(jnp.int32, (width, 1), 0))
    first_col = position() * 2
    m0, m1 = live(counts, 0), live(counts, 1)

    def placed(step):
        e = exc[step]
        return jnp.where(col == first_col, e[0:1], jnp.where(col == first_col + 1, e[1:2], 0.0))

    h0, h1 = permuted(hist[0], order[...]), permuted(hist[1], order[...])
    p0 = dot(r0[...], h0) * m0
    copies[0].wait()
    p0 += dot(r1[...], h1) * m1
    d0 = (placed(0) - p0.T).astype(BF16)
    d0_ref[...] = d0
    copies[1].wait()
    first = dot_t(d0, inv_v[...]).astype(BF16)
    trace = dot(first, select[...]).astype(BF16)
    down_ref[...] = trace[:, :half]
    up_ref[...] = trace[:, half:]
    d1_ref[...] = placed(1) - (dot(r1[...], h0) * m1).T


def pack_partials(counts, order, d0, d1, up, down, r0, before, hist, out, h0_ref):
    h0_ref[...] = hist[0]
    n = d0.shape[1]
    half = up.shape[1]
    out[:, :n] = d0[...]
    out[:, n : n + half] = up[...]
    out[:, n + half : n + 2 * half] = down[...]
    p1 = dot(r0[...], permuted(before[...], order[...])) * live(counts, 0)
    out[:, n + 2 * half :] = (d1[...] - p1.T).astype(BF16)


def sum_parts(x, out):
    total = x[0].astype(F32)
    for i in range(1, x.shape[0]):
        total += x[i].astype(F32)
    out[...] = total


def two_firsts(counts, x0, x1, x2, x3, inv, tra, select, r0_even, r0_odd, cur_ref, first_ref, up_ref, down_ref, r0, sem):
    odd = lax.axis_index("c") == 1

    @pl.when(odd)
    def _():
        copied(r0_odd, r0, sem)

    @pl.when(jnp.logical_not(odd))
    def _():
        copied(r0_even, r0, sem)

    n = inv.shape[0]
    faces_count = select.shape[1]
    half = faces_count // 2
    total = (x0[...] + x1[...]) + (x2[...] + x3[...])
    rhs = total[:, :n].astype(BF16)
    neighbour = total[:, n : n + faces_count].astype(BF16)
    d1 = total[:, n + faces_count :]
    coupling = dot_t(neighbour, tra[...]).astype(BF16)
    cur = dot_t(rhs, inv[...]) - dot_t(coupling, inv[...])
    cur_ref[...] = cur
    alive = (counts[0] > 0).astype(F32)
    newest = dot_t(cur.astype(BF16), r0[...]) * alive
    first = dot_t((d1 - newest).astype(BF16), inv[...])
    first_ref[...] = first
    trace = dot(first.astype(BF16), select[...]).astype(BF16)
    down_ref[...] = trace[:, :half]
    up_ref[...] = trace[:, half:]


def second_current(cur0, first, up, down, inv, tra, gather_ref, *share_refs):
    half = up.shape[1]
    coupling = dot_t(up[...], tra[:, :half]) + dot_t(down[...], tra[:, half:])
    cur1 = first[...] - dot_t(coupling.astype(BF16), inv[...])
    c0 = cur0[...]
    both = jnp.concatenate([cur1.astype(BF16), c0.astype(BF16)], axis=0)
    for i in range(gather_ref.shape[0]):
        gather_ref[i] = both
    for i, share in enumerate(share_refs):
        share[0] = c0[2 * i : 2 * i + 2]
        share[1] = cur1[2 * i : 2 * i + 2]


def finish(gathered, s0, s1, s2, s3, before0, before1, cur_ref, hist_ref):
    zh = lax.axis_index("zh")
    cur_ref[...] = jnp.where(zh < 2, jnp.where(zh == 0, s0[...], s1[...]), jnp.where(zh == 2, s2[...], s3[...]))
    leading = position() == 0

    @pl.when(leading)
    def _():
        owners, cols = gathered.shape[0], gathered.shape[1] // 2
        order = permutation(owners * cols)
        for slot in range(2):
            both = gathered[:, slot * cols : (slot + 1) * cols, :].reshape(owners * cols, -1)
            hist_ref[slot] = dot_t(both.astype(F32).T.astype(BF16), order).astype(BF16)

    @pl.when(jnp.logical_not(leading))
    def _():
        hist_ref[0] = before0[...]
        hist_ref[1] = before1[...]


def relay(held_at, first_at, held, first, second, after, out, sem):
    y = lax.axis_index("y")
    holds, from_first = one_of(y, held_at), one_of(y, first_at)

    @pl.when(holds)
    def _():
        copied(held, out, sem)

    @pl.when(jnp.logical_and(jnp.logical_not(holds), from_first))
    def _():
        copied(first, out, sem)

    @pl.when(jnp.logical_not(jnp.logical_or(holds, from_first)))
    def _():
        copied(second, out, sem)


def one_of(value, members):
    found = value == members[0]
    for member in members[1:]:
        found = jnp.logical_or(found, value == member)
    return found


def permute(value, axes, pairs):
    return lax.ppermute(value, axes, pairs)


def body(excitation, retarded, history, inverse, transfer, faces, counts):
    slots, n, width = history.shape
    steps = excitation.shape[0]
    half = faces.shape[1] // 2
    devices = Y * ZH * CORE
    cols = width // OWNERS
    exc = jnp.transpose(excitation, (0, 2, 1))
    any_spec = pl.BlockSpec(memory_space=pl.ANY)

    def at(yy, z, c):
        return (yy * ZH + z) * CORE + c

    def spread(value, *hops):
        return permute(value, DELAY, [(at(i, 0, 0), at(j, 0, 0)) for i, j in hops])

    def relayed(held_at, first_at, *operands):
        return call(
            functools.partial(relay, held_at, first_at),
            shape((n, n), BF16),
            [any_spec] * 4,
            0,
            1024 * 1024,
            scratch_shapes=[pltpu.SemaphoreType.DMA],
        )(*operands)

    ring = [(i, (i + 1) % DOM) for i in range(DOM)]
    back = [(j, i) for i, j in ring]
    chain = [(i, i + 1) for i in range(devices - 1)]

    macs = n * n * width
    select, order, r0, h1 = call(
        selections,
        (shape((n, 2 * half), BF16), shape((width, width), BF16), shape((n, n), BF16), shape((n, width), BF16)),
        [VMEM] + [any_spec] * 2,
        0,
        1024 * 1024,
        mib=52,
        scratch_shapes=[pltpu.SemaphoreType.DMA((2,))],
    )(faces, retarded, history)
    before1 = permute(h1, DELAY, chain)
    s1a, s1b = spread(r0, (0, 3)), spread(r0, (0, 5))
    d0, d1, up, down = call(
        own_partials,
        (shape((width, n), BF16), shape((width, n), F32), shape((width, half), BF16), shape((width, half), BF16)),
        [SMEM] + [VMEM] * 5 + [any_spec] * 2,
        2 * macs * 4,
        2 * 1024 * 1024,
        mib=52,
        scratch_shapes=[pltpu.VMEM((n, n), BF16), pltpu.VMEM((n, n), BF16), pltpu.SemaphoreType.DMA((2,))],
    )(counts, exc, select, order, history, r0, retarded, inverse)
    up = permute(up, "dom", ring)
    down = permute(down, "dom", back)
    lanes = 2 * n + 2 * half
    packed, h0 = call(
        pack_partials,
        (shape((width, lanes), BF16), shape((n, width), BF16)),
        [SMEM] + [VMEM] * 8,
        2 * macs,
        1024 * 1024,
    )(counts, order, d0, d1, up, down, r0, before1, history)
    x = lax.all_to_all(packed.reshape(OWNERS, cols, lanes), ("y", "c"), 0, 0, tiled=True)
    before0 = permute(h0, DELAY, chain)
    r0 = relayed((0,), (3,), r0, s1a, s1b, packed)
    s2a, s2b = spread(r0, (0, 1), (3, 2), (5, 6)), spread(r0, (0, 7), (3, 4))
    x = call(sum_parts, shape((cols, lanes), F32), [VMEM], 0, 512 * 1024)(x)
    xs = [x] + [permute(x, "zh", [(z, 0)]) for z in range(1, ZH)]
    r0 = relayed((0, 3, 5), (1, 2, 6), r0, s2a, s2b, x)
    s3 = permute(r0, DELAY, [(at(i, 0, 0), at(i, 0, 1)) for i in range(Y)])

    cur0, first, up, down = call(
        two_firsts,
        (shape((cols, n), F32), shape((cols, n), F32), shape((cols, half), BF16), shape((cols, half), BF16)),
        [SMEM] + [VMEM] * 7 + [any_spec] * 2,
        2 * 8 * n * n * 6,
        2 * 1024 * 1024,
        scratch_shapes=[pltpu.VMEM((n, n), BF16), pltpu.SemaphoreType.DMA],
    )(counts, *xs, inverse, transfer, select, r0, s3)
    up = permute(up, ("zh", "dom"), ring)
    down = permute(down, ("zh", "dom"), back)
    gather, *share = call(
        second_current,
        [shape((OWNERS, 2 * cols, n), BF16)] + [shape((steps, 2, n), F32)] * ZH,
        [VMEM] * 6,
        2 * 8 * n * n * 2,
        1024 * 1024,
    )(cur0, first, up, down, inverse, transfer)
    gather = lax.all_to_all(gather, ("y", "c"), 0, 0, tiled=True)
    for z in range(1, ZH):
        share[z] = permute(share[z], DELAY, [(at(i, 0, c), at(i, z, c)) for i in range(Y) for c in range(CORE)])
    currents, new_history = call(
        finish,
        (shape((steps, 2, n), F32), shape(history.shape, BF16)),
        [VMEM] * 7,
        0,
        1024 * 1024,
    )(gather, *share, before0, before1)
    return jnp.transpose(currents, (0, 2, 1)), new_history


def solution(mesh):
    split = Mesh(mesh.devices.reshape(Y, ZH, CORE, DOM), ("y", "zh", "c", "dom"))
    placed = (
        P(None, "dom", DELAY),
        P(DELAY, "dom", None),
        P(DELAY, "dom", None),
        P("dom", None),
        P("dom", None),
        P("dom", None),
        P("dom"),
    )
    return jax.shard_map(
        body,
        mesh=split,
        in_specs=placed,
        out_specs=(P(None, "dom", DELAY), P(DELAY, "dom", None)),
        check_vma=False,
    )
```

```python
import functools

import jax
import jax.numpy as jnp
from jax import lax
from jax.experimental import pallas as pl
from jax.experimental.pallas import tpu as pltpu
from jax.sharding import Mesh, PartitionSpec as P

Y, ZH, CORE, DOM = 8, 4, 2, 8
OWNERS = Y * CORE
DELAY = ("y", "zh", "c")
F32, BF16 = jnp.float32, jnp.bfloat16
VMEM = pl.BlockSpec(memory_space=pltpu.VMEM)
SMEM = pl.BlockSpec(memory_space=pltpu.SMEM)


def call(kernel, out_shape, in_specs, flops, nbytes, mib=32, out_specs=None, **more):
    if out_specs is None:
        out_specs = jax.tree.map(lambda _: VMEM, out_shape)
    return pl.pallas_call(
        kernel,
        out_shape=out_shape,
        in_specs=in_specs,
        out_specs=out_specs,
        compiler_params=pltpu.CompilerParams(vmem_limit_bytes=mib * 1024 * 1024),
        cost_estimate=pl.CostEstimate(flops=flops, bytes_accessed=nbytes, transcendentals=0),
        **more,
    )


def shape(dims, dtype):
    return jax.ShapeDtypeStruct(dims, dtype)


def dot(a, b):
    return jnp.dot(a, b, preferred_element_type=F32)


def dot_t(a, b):
    return lax.dot_general(a, b, (((1,), (1,)), ((), ())), preferred_element_type=F32)


def one_hot_rows(faces, rows):
    ids = lax.broadcasted_iota(jnp.int32, (rows, faces.shape[1]), 0)
    return (ids == faces).astype(F32).astype(BF16)


def position():
    return (lax.axis_index("y") * ZH + lax.axis_index("zh")) * CORE + lax.axis_index("c")


def live(counts, slot):
    return (position() * 2 + slot < counts[0]).astype(F32)


def copied(source, target, sem):
    copy = pltpu.make_async_copy(source, target, sem)
    copy.start()
    copy.wait()


def column_of(row):
    c, zh = (row // 8) % 2, (row // 2) % 4
    return (row // 16) * 16 + zh * 4 + c * 2 + row % 2


def permutation(width):
    cols = lax.broadcasted_iota(jnp.int32, (width, width), 0)
    rows = lax.broadcasted_iota(jnp.int32, (width, width), 1)
    return (cols == column_of(rows)).astype(F32).astype(BF16)


def permuted(block, order):
    return dot(block, order).astype(BF16)


def selections(faces, ret, hist, select_ref, order_ref, r0_ref, h1_ref, sems):
    moves = [(hist.at[hist.shape[0] - 1], h1_ref), (ret.at[0], r0_ref)]
    copies = [pltpu.make_async_copy(a, b, sems.at[k]) for k, (a, b) in enumerate(moves)]
    for copy in copies:
        copy.start()
    select_ref[...] = one_hot_rows(faces[...], select_ref.shape[0])
    order_ref[...] = permutation(order_ref.shape[0])
    for copy in copies:
        copy.wait()


def own_partials(counts, exc, order, hist, r0, ret, d0_ref, d1_ref, r1, sem):
    copy = pltpu.make_async_copy(ret.at[1], r1, sem)
    copy.start()
    width = hist.shape[2]
    col = column_of(lax.broadcasted_iota(jnp.int32, (width, 1), 0))
    first_col = position() * 2
    m0, m1 = live(counts, 0), live(counts, 1)

    def placed(step):
        e = exc[step]
        return jnp.where(col == first_col, e[0:1], jnp.where(col == first_col + 1, e[1:2], 0.0))

    h0, h1 = permuted(hist[0], order[...]), permuted(hist[1], order[...])
    p0 = dot(r0[...], h0) * m0
    copy.wait()
    p0 += dot(r1[...], h1) * m1
    d0_ref[...] = (placed(0) - p0.T).astype(BF16)
    d1_ref[...] = placed(1) - (dot(r1[...], h0) * m1).T


def pack_partials(counts, order, d0, d1, r0, before, hist, out, h0_ref):
    h0_ref[...] = hist[0]
    n = d0.shape[1]
    out[:, :n] = d0[...]
    p1 = dot(r0[...], permuted(before[...], order[...])) * live(counts, 0)
    out[:, n:] = (d1[...] - p1.T).astype(BF16)


def sum_parts(x, out):
    total = x[0].astype(F32)
    for i in range(1, x.shape[0]):
        total += x[i].astype(F32)
    out[...] = total


def trace_of(first, select, up_ref, down_ref):
    trace = dot(first.astype(BF16), select[...]).astype(BF16)
    half = select.shape[1] // 2
    down_ref[...] = trace[:, :half]
    up_ref[...] = trace[:, half:]


def coupled(up, down, inv, tra):
    half = up.shape[1]
    coupling = dot_t(up[...], tra[:, :half]) + dot_t(down[...], tra[:, half:])
    return dot_t(coupling.astype(BF16), inv[...])


def first_of_sum(x0, x1, x2, x3, inv, select, first_ref, rest_ref, up_ref, down_ref):
    n = inv.shape[0]
    total = (x0[...] + x1[...]) + (x2[...] + x3[...])
    first = dot_t(total[:, :n].astype(BF16), inv[...])
    first_ref[...] = first
    rest_ref[...] = total[:, n:]
    trace_of(first, select, up_ref, down_ref)


def next_first(
    counts, first, rest, up, down, inv, tra, select, r0_even, r0_odd,
    cur_ref, first_ref, up_ref, down_ref,
    r0, sem,
):
    odd = lax.axis_index("c") == 1

    @pl.when(odd)
    def _():
        copied(r0_odd, r0, sem)

    @pl.when(jnp.logical_not(odd))
    def _():
        copied(r0_even, r0, sem)

    cur = first[...] - coupled(up, down, inv, tra)
    cur_ref[...] = cur
    alive = (counts[0] > 0).astype(F32)
    newest = dot_t(cur.astype(BF16), r0[...]) * alive
    following = dot_t((rest[...] - newest).astype(BF16), inv[...])
    first_ref[...] = following
    trace_of(following, select, up_ref, down_ref)


def second_current(cur0, first, up, down, inv, tra, gather_ref, *share_refs):
    cur1 = first[...] - coupled(up, down, inv, tra)
    c0 = cur0[...]
    both = jnp.concatenate([cur1.astype(BF16), c0.astype(BF16)], axis=0)
    for i in range(gather_ref.shape[0]):
        gather_ref[i] = both
    for i, share in enumerate(share_refs):
        share[0] = c0[2 * i : 2 * i + 2]
        share[1] = cur1[2 * i : 2 * i + 2]


def finish(gathered, s0, s1, s2, s3, before0, before1, cur_ref, hist_ref):
    zh = lax.axis_index("zh")
    cur_ref[...] = jnp.where(zh < 2, jnp.where(zh == 0, s0[...], s1[...]), jnp.where(zh == 2, s2[...], s3[...]))
    leading = position() == 0

    @pl.when(leading)
    def _():
        owners, cols = gathered.shape[0], gathered.shape[1] // 2
        order = permutation(owners * cols)
        for slot in range(2):
            both = gathered[:, slot * cols : (slot + 1) * cols, :].reshape(owners * cols, -1)
            hist_ref[slot] = dot_t(both.astype(F32).T.astype(BF16), order).astype(BF16)

    @pl.when(jnp.logical_not(leading))
    def _():
        hist_ref[0] = before0[...]
        hist_ref[1] = before1[...]


def relay(held_at, first_at, held, first, second, after, out, sem):
    y = lax.axis_index("y")
    holds, from_first = one_of(y, held_at), one_of(y, first_at)

    @pl.when(holds)
    def _():
        copied(held, out, sem)

    @pl.when(jnp.logical_and(jnp.logical_not(holds), from_first))
    def _():
        copied(first, out, sem)

    @pl.when(jnp.logical_not(jnp.logical_or(holds, from_first)))
    def _():
        copied(second, out, sem)


def one_of(value, members):
    found = value == members[0]
    for member in members[1:]:
        found = jnp.logical_or(found, value == member)
    return found


def permute(value, axes, pairs):
    return lax.ppermute(value, axes, pairs)


def body(excitation, retarded, history, inverse, transfer, faces, counts):
    slots, n, width = history.shape
    steps = excitation.shape[0]
    half = faces.shape[1] // 2
    devices = Y * ZH * CORE
    cols = width // OWNERS
    exc = jnp.transpose(excitation, (0, 2, 1))
    any_spec = pl.BlockSpec(memory_space=pl.ANY)

    def at(yy, z, c):
        return (yy * ZH + z) * CORE + c

    def spread(value, *hops):
        return permute(value, DELAY, [(at(i, 0, 0), at(j, 0, 0)) for i, j in hops])

    def relayed(held_at, first_at, *operands):
        return call(
            functools.partial(relay, held_at, first_at),
            shape((n, n), BF16),
            [any_spec] * 4,
            0,
            1024 * 1024,
            scratch_shapes=[pltpu.SemaphoreType.DMA],
        )(*operands)

    ring = [(i, (i + 1) % DOM) for i in range(DOM)]
    back = [(j, i) for i, j in ring]
    chain = [(i, i + 1) for i in range(devices - 1)]

    macs = n * n * width
    select, order, r0, h1 = call(
        selections,
        (shape((n, 2 * half), BF16), shape((width, width), BF16), shape((n, n), BF16), shape((n, width), BF16)),
        [VMEM] + [any_spec] * 2,
        0,
        1024 * 1024,
        mib=52,
        scratch_shapes=[pltpu.SemaphoreType.DMA((2,))],
    )(faces, retarded, history)
    before1 = permute(h1, DELAY, chain)
    d0, d1 = call(
        own_partials,
        (shape((width, n), BF16), shape((width, n), F32)),
        [SMEM] + [VMEM] * 4 + [any_spec],
        2 * macs * 4,
        2 * 1024 * 1024,
        mib=52,
        scratch_shapes=[pltpu.VMEM((n, n), BF16), pltpu.SemaphoreType.DMA],
    )(counts, exc, order, history, r0, retarded)
    s1a, s1b = spread(r0, (0, 3)), spread(r0, (0, 5))
    lanes = 2 * n
    packed, h0 = call(
        pack_partials,
        (shape((width, lanes), BF16), shape((n, width), BF16)),
        [SMEM] + [VMEM] * 6,
        2 * macs,
        1024 * 1024,
    )(counts, order, d0, d1, r0, before1, history)
    before0 = permute(h0, DELAY, chain)
    x = lax.all_to_all(packed.reshape(OWNERS, cols, lanes), ("y", "c"), 0, 0, tiled=True)
    r0 = relayed((0,), (3,), r0, s1a, s1b, packed)
    s2a, s2b = spread(r0, (0, 1), (3, 2), (5, 6)), spread(r0, (0, 7), (3, 4))
    x = call(sum_parts, shape((cols, lanes), F32), [VMEM], 0, 512 * 1024)(x)
    xs = [x] + [permute(x, "zh", [(z, 0)]) for z in range(1, ZH)]

    def halo(up, down):
        return permute(up, ("zh", "dom"), ring), permute(down, ("zh", "dom"), back)

    trace_shape = (shape((cols, half), BF16),) * 2
    first, rest, up, down = call(
        first_of_sum,
        (shape((cols, n), F32), shape((cols, n), F32)) + trace_shape,
        [VMEM] * 6,
        2 * 8 * n * n * 2,
        1024 * 1024,
    )(*xs, inverse, select)
    r0 = relayed((0, 3, 5), (1, 2, 6), r0, s2a, s2b, rest)
    s3 = permute(r0, DELAY, [(at(i, 0, 0), at(i, 0, 1)) for i in range(Y)])
    up, down = halo(up, down)
    cur0, first, up, down = call(
        next_first,
        (shape((cols, n), F32), shape((cols, n), F32)) + trace_shape,
        [SMEM] + [VMEM] * 7 + [any_spec] * 2,
        2 * 8 * n * n * 5,
        2 * 1024 * 1024,
        scratch_shapes=[pltpu.VMEM((n, n), BF16), pltpu.SemaphoreType.DMA],
    )(counts, first, rest, up, down, inverse, transfer, select, r0, s3)
    up, down = halo(up, down)
    gather, *share = call(
        second_current,
        [shape((OWNERS, 2 * cols, n), BF16)] + [shape((steps, 2, n), F32)] * ZH,
        [VMEM] * 6,
        2 * 8 * n * n * 2,
        1024 * 1024,
    )(cur0, first, up, down, inverse, transfer)
    gather = lax.all_to_all(gather, ("y", "c"), 0, 0, tiled=True)
    for z in range(1, ZH):
        share[z] = permute(share[z], DELAY, [(at(i, 0, c), at(i, z, c)) for i in range(Y) for c in range(CORE)])
    currents, new_history = call(
        finish,
        (shape((steps, 2, n), F32), shape(history.shape, BF16)),
        [VMEM] * 7,
        0,
        1024 * 1024,
    )(gather, *share, before0, before1)
    return jnp.transpose(currents, (0, 2, 1)), new_history


def solution(mesh):
    split = Mesh(mesh.devices.reshape(Y, ZH, CORE, DOM), ("y", "zh", "c", "dom"))
    placed = (
        P(None, "dom", DELAY),
        P(DELAY, "dom", None),
        P(DELAY, "dom", None),
        P("dom", None),
        P("dom", None),
        P("dom", None),
        P("dom"),
    )
    return jax.shard_map(
        body,
        mesh=split,
        in_specs=placed,
        out_specs=(P(None, "dom", DELAY), P(DELAY, "dom", None)),
        check_vma=False,
    )
```

```python
import functools

import jax
import jax.numpy as jnp
from jax import lax
from jax.experimental import pallas as pl
from jax.experimental.pallas import tpu as pltpu
from jax.sharding import Mesh, PartitionSpec as P

Y, ZH, CORE, DOM = 8, 4, 2, 8
OWNERS = Y * CORE
DELAY = ("y", "zh", "c")
F32, BF16 = jnp.float32, jnp.bfloat16
VMEM = pl.BlockSpec(memory_space=pltpu.VMEM)
SMEM = pl.BlockSpec(memory_space=pltpu.SMEM)


def call(kernel, out_shape, in_specs, flops, nbytes, mib=32, out_specs=None, **more):
    if out_specs is None:
        out_specs = jax.tree.map(lambda _: VMEM, out_shape)
    return pl.pallas_call(
        kernel,
        out_shape=out_shape,
        in_specs=in_specs,
        out_specs=out_specs,
        compiler_params=pltpu.CompilerParams(vmem_limit_bytes=mib * 1024 * 1024),
        cost_estimate=pl.CostEstimate(flops=flops, bytes_accessed=nbytes, transcendentals=0),
        **more,
    )


def shape(dims, dtype):
    return jax.ShapeDtypeStruct(dims, dtype)


def dot(a, b):
    return jnp.dot(a, b, preferred_element_type=F32)


def dot_t(a, b):
    return lax.dot_general(a, b, (((1,), (1,)), ((), ())), preferred_element_type=F32)


def one_hot_rows(faces, rows):
    ids = lax.broadcasted_iota(jnp.int32, (rows, faces.shape[1]), 0)
    return (ids == faces).astype(F32).astype(BF16)


def position():
    return (lax.axis_index("y") * ZH + lax.axis_index("zh")) * CORE + lax.axis_index("c")


def live(counts, slot):
    return (position() * 2 + slot < counts[0]).astype(F32)


def copied(source, target, sem):
    copy = pltpu.make_async_copy(source, target, sem)
    copy.start()
    copy.wait()


def column_of(row):
    c, zh = (row // 8) % 2, (row // 2) % 4
    return (row // 16) * 16 + zh * 4 + c * 2 + row % 2


def permutation(width):
    cols = lax.broadcasted_iota(jnp.int32, (width, width), 0)
    rows = lax.broadcasted_iota(jnp.int32, (width, width), 1)
    return (cols == column_of(rows)).astype(F32).astype(BF16)


def permuted(block, order):
    return dot(block, order).astype(BF16)


def first_blocks(ret, hist, r0_ref, h1_ref, sems):
    moves = [(hist.at[hist.shape[0] - 1], h1_ref), (ret.at[0], r0_ref)]
    copies = [pltpu.make_async_copy(a, b, sems.at[k]) for k, (a, b) in enumerate(moves)]
    for copy in copies:
        copy.start()
    for copy in copies:
        copy.wait()


def own_partials(counts, exc, faces, hist, r0, ret, d0_ref, d1_ref, select_ref, order_ref, r1, sem):
    copy = pltpu.make_async_copy(ret.at[1], r1, sem)
    copy.start()
    width = hist.shape[2]
    col = column_of(lax.broadcasted_iota(jnp.int32, (width, 1), 0))
    first_col = position() * 2
    m0, m1 = live(counts, 0), live(counts, 1)

    def placed(step):
        e = exc[step]
        return jnp.where(col == first_col, e[0:1], jnp.where(col == first_col + 1, e[1:2], 0.0))

    order = permutation(width)
    order_ref[...] = order
    select_ref[...] = one_hot_rows(faces[...], select_ref.shape[0])
    h0, h1 = permuted(hist[0], order), permuted(hist[1], order)
    p0 = dot(r0[...], h0) * m0
    copy.wait()
    p0 += dot(r1[...], h1) * m1
    d0_ref[...] = (placed(0) - p0.T).astype(BF16)
    d1_ref[...] = placed(1) - (dot(r1[...], h0) * m1).T


def pack_partials(counts, order, d0, d1, r0, before, hist, out, h0_ref):
    h0_ref[...] = hist[0]
    n = d0.shape[1]
    out[:, :n] = d0[...]
    p1 = dot(r0[...], permuted(before[...], order[...])) * live(counts, 0)
    out[:, n:] = (d1[...] - p1.T).astype(BF16)


def sum_parts(x, out, sent):
    total = x[0].astype(F32)
    for i in range(1, x.shape[0]):
        total += x[i].astype(F32)
    out[...] = total
    sent[...] = total.astype(BF16)


def send_traces(first, select, out):
    trace = dot(first.astype(BF16), select[...]).astype(BF16)
    half = select.shape[1] // 2
    dom = lax.axis_index("dom")
    out[...] = jnp.zeros_like(out)
    out[(dom + 1) % DOM] = trace[:, half:]
    out[(dom + DOM - 1) % DOM] = trace[:, :half]


def coupled(traces, inv, tra):
    half = traces.shape[2]
    dom = lax.axis_index("dom")
    up, down = traces[(dom + DOM - 1) % DOM], traces[(dom + 1) % DOM]
    coupling = dot_t(up, tra[:, :half]) + dot_t(down, tra[:, half:])
    return dot_t(coupling.astype(BF16), inv[...])


def first_of_sum(x0, x1, x2, x3, inv, select, first_ref, rest_ref, traces_ref):
    n = inv.shape[0]
    total = (x0[...] + x1[...].astype(F32)) + (x2[...].astype(F32) + x3[...].astype(F32))
    first = dot_t(total[:, :n].astype(BF16), inv[...])
    first_ref[...] = first
    rest_ref[...] = total[:, n:]
    send_traces(first, select, traces_ref)


def next_first(
    counts, first, rest, traces, inv, tra, select, r0_even, r0_odd,
    cur_ref, first_ref, traces_ref,
    r0, sem,
):
    odd = lax.axis_index("c") == 1

    @pl.when(odd)
    def _():
        copied(r0_odd, r0, sem)

    @pl.when(jnp.logical_not(odd))
    def _():
        copied(r0_even, r0, sem)

    cur = first[...] - coupled(traces, inv, tra)
    cur_ref[...] = cur
    alive = (counts[0] > 0).astype(F32)
    newest = dot_t(cur.astype(BF16), r0[...]) * alive
    following = dot_t((rest[...] - newest).astype(BF16), inv[...])
    first_ref[...] = following
    send_traces(following, select, traces_ref)


def second_current(cur0, first, traces, inv, tra, gather_ref, *share_refs):
    cur1 = first[...] - coupled(traces, inv, tra)
    c0 = cur0[...]
    both = jnp.concatenate([cur1.astype(BF16), c0.astype(BF16)], axis=0)
    for i in range(gather_ref.shape[0]):
        gather_ref[i] = both
    for i, share in enumerate(share_refs):
        share[0] = c0[2 * i : 2 * i + 2]
        share[1] = cur1[2 * i : 2 * i + 2]


def finish(gathered, s0, s1, s2, s3, before0, before1, cur_ref, hist_ref):
    zh = lax.axis_index("zh")
    cur_ref[...] = jnp.where(zh < 2, jnp.where(zh == 0, s0[...], s1[...]), jnp.where(zh == 2, s2[...], s3[...]))
    leading = position() == 0

    @pl.when(leading)
    def _():
        owners, cols = gathered.shape[0], gathered.shape[1] // 2
        order = permutation(owners * cols)
        for slot in range(2):
            both = gathered[:, slot * cols : (slot + 1) * cols, :].reshape(owners * cols, -1)
            hist_ref[slot] = dot_t(both.astype(F32).T.astype(BF16), order).astype(BF16)

    @pl.when(jnp.logical_not(leading))
    def _():
        hist_ref[0] = before0[...]
        hist_ref[1] = before1[...]


def relay(held_at, first_at, held, first, second, after, out, sem):
    y = lax.axis_index("y")
    holds, from_first = one_of(y, held_at), one_of(y, first_at)

    @pl.when(holds)
    def _():
        copied(held, out, sem)

    @pl.when(jnp.logical_and(jnp.logical_not(holds), from_first))
    def _():
        copied(first, out, sem)

    @pl.when(jnp.logical_not(jnp.logical_or(holds, from_first)))
    def _():
        copied(second, out, sem)


def one_of(value, members):
    found = value == members[0]
    for member in members[1:]:
        found = jnp.logical_or(found, value == member)
    return found


def permute(value, axes, pairs):
    return lax.ppermute(value, axes, pairs)


def body(excitation, retarded, history, inverse, transfer, faces, counts):
    slots, n, width = history.shape
    steps = excitation.shape[0]
    half = faces.shape[1] // 2
    devices = Y * ZH * CORE
    cols = width // OWNERS
    exc = jnp.transpose(excitation, (0, 2, 1))
    any_spec = pl.BlockSpec(memory_space=pl.ANY)

    def at(yy, z, c):
        return (yy * ZH + z) * CORE + c

    def spread(value, *hops):
        return permute(value, DELAY, [(at(i, 0, 0), at(j, 0, 0)) for i, j in hops])

    def relayed(held_at, first_at, *operands):
        return call(
            functools.partial(relay, held_at, first_at),
            shape((n, n), BF16),
            [any_spec] * 4,
            0,
            1024 * 1024,
            scratch_shapes=[pltpu.SemaphoreType.DMA],
        )(*operands)

    chain = [(i, i + 1) for i in range(devices - 1)]

    macs = n * n * width
    r0, h1 = call(
        first_blocks,
        (shape((n, n), BF16), shape((n, width), BF16)),
        [any_spec] * 2,
        0,
        1024 * 1024,
        mib=53,
        scratch_shapes=[pltpu.SemaphoreType.DMA((2,))],
    )(retarded, history)
    before1 = permute(h1, DELAY, chain)
    d0, d1, select, order = call(
        own_partials,
        (shape((width, n), BF16), shape((width, n), F32), shape((n, 2 * half), BF16), shape((width, width), BF16)),
        [SMEM] + [VMEM] * 4 + [any_spec],
        2 * macs * 4,
        2 * 1024 * 1024,
        mib=52,
        scratch_shapes=[pltpu.VMEM((n, n), BF16), pltpu.SemaphoreType.DMA],
    )(counts, exc, faces, history, r0, retarded)
    s1a, s1b = spread(r0, (0, 3)), spread(r0, (0, 5))
    lanes = 2 * n
    packed, h0 = call(
        pack_partials,
        (shape((width, lanes), BF16), shape((n, width), BF16)),
        [SMEM] + [VMEM] * 6,
        2 * macs,
        1024 * 1024,
    )(counts, order, d0, d1, r0, before1, history)
    before0 = permute(h0, DELAY, chain)
    x = lax.all_to_all(packed.reshape(OWNERS, cols, lanes), ("y", "c"), 0, 0, tiled=True)
    r0 = relayed((0,), (3,), r0, s1a, s1b, packed)
    s2a, s2b = spread(r0, (0, 1), (3, 2), (5, 6)), spread(r0, (0, 7), (3, 4))
    x, sent = call(
        sum_parts, (shape((cols, lanes), F32), shape((cols, lanes), BF16)), [VMEM], 0, 512 * 1024
    )(x)
    xs = [x] + [permute(sent, "zh", [(z, 0)]) for z in range(1, ZH)]

    def halo(traces):
        return lax.all_to_all(traces, "dom", 0, 0, tiled=True)

    owned = shape((cols, n), F32)
    traces_shape = shape((DOM, cols, half), BF16)
    first, rest, traces = call(
        first_of_sum,
        (owned, owned, traces_shape),
        [VMEM] * 6,
        2 * 8 * n * n * 2,
        1024 * 1024,
    )(*xs, inverse, select)
    r0 = relayed((0, 3, 5), (1, 2, 6), r0, s2a, s2b, rest)
    s3 = permute(r0, DELAY, [(at(i, 0, 0), at(i, 0, 1)) for i in range(Y)])
    traces = halo(traces)
    cur0, first, traces = call(
        next_first,
        (owned, owned, traces_shape),
        [SMEM] + [VMEM] * 6 + [any_spec] * 2,
        2 * 8 * n * n * 5,
        2 * 1024 * 1024,
        scratch_shapes=[pltpu.VMEM((n, n), BF16), pltpu.SemaphoreType.DMA],
    )(counts, first, rest, traces, inverse, transfer, select, r0, s3)
    traces = halo(traces)
    gather, *share = call(
        second_current,
        [shape((OWNERS, 2 * cols, n), BF16)] + [shape((steps, 2, n), F32)] * ZH,
        [VMEM] * 5,
        2 * 8 * n * n * 2,
        1024 * 1024,
    )(cur0, first, traces, inverse, transfer)
    gather = lax.all_to_all(gather, ("y", "c"), 0, 0, tiled=True)
    for z in range(1, ZH):
        share[z] = permute(share[z], DELAY, [(at(i, 0, c), at(i, z, c)) for i in range(Y) for c in range(CORE)])
    currents, new_history = call(
        finish,
        (shape((steps, 2, n), F32), shape(history.shape, BF16)),
        [VMEM] * 7,
        0,
        1024 * 1024,
    )(gather, *share, before0, before1)
    return jnp.transpose(currents, (0, 2, 1)), new_history


def solution(mesh):
    split = Mesh(mesh.devices.reshape(Y, ZH, CORE, DOM), ("y", "zh", "c", "dom"))
    placed = (
        P(None, "dom", DELAY),
        P(DELAY, "dom", None),
        P(DELAY, "dom", None),
        P("dom", None),
        P("dom", None),
        P("dom", None),
        P("dom"),
    )
    return jax.shard_map(
        body,
        mesh=split,
        in_specs=placed,
        out_specs=(P(None, "dom", DELAY), P(DELAY, "dom", None)),
        check_vma=False,
    )
```

```python
import functools

import jax
import jax.numpy as jnp
from jax import lax
from jax.experimental import pallas as pl
from jax.experimental.pallas import tpu as pltpu
from jax.sharding import Mesh, PartitionSpec as P

Y, ZH, CORE, DOM = 8, 4, 2, 8
OWNERS = Y * CORE
DELAY = ("y", "zh", "c")
F32, BF16 = jnp.float32, jnp.bfloat16
VMEM = pl.BlockSpec(memory_space=pltpu.VMEM)
SMEM = pl.BlockSpec(memory_space=pltpu.SMEM)


def call(kernel, out_shape, in_specs, flops, nbytes, mib=32, out_specs=None, **more):
    if out_specs is None:
        out_specs = jax.tree.map(lambda _: VMEM, out_shape)
    return pl.pallas_call(
        kernel,
        out_shape=out_shape,
        in_specs=in_specs,
        out_specs=out_specs,
        compiler_params=pltpu.CompilerParams(vmem_limit_bytes=mib * 1024 * 1024),
        cost_estimate=pl.CostEstimate(flops=flops, bytes_accessed=nbytes, transcendentals=0),
        **more,
    )


def shape(dims, dtype):
    return jax.ShapeDtypeStruct(dims, dtype)


def dot(a, b):
    return jnp.dot(a, b, preferred_element_type=F32)


def dot_t(a, b):
    return lax.dot_general(a, b, (((1,), (1,)), ((), ())), preferred_element_type=F32)


def one_hot_rows(faces, rows):
    ids = lax.broadcasted_iota(jnp.int32, (rows, faces.shape[1]), 0)
    return (ids == faces).astype(F32).astype(BF16)


def position():
    return (lax.axis_index("y") * ZH + lax.axis_index("zh")) * CORE + lax.axis_index("c")


def live(counts, slot):
    return (position() * 2 + slot < counts[0]).astype(F32)


def copied(source, target, sem):
    copy = pltpu.make_async_copy(source, target, sem)
    copy.start()
    copy.wait()


def column_of(row):
    c, zh = (row // 8) % 2, (row // 2) % 4
    return (row // 16) * 16 + zh * 4 + c * 2 + row % 2


def permutation(width):
    cols = lax.broadcasted_iota(jnp.int32, (width, width), 0)
    rows = lax.broadcasted_iota(jnp.int32, (width, width), 1)
    return (cols == column_of(rows)).astype(F32).astype(BF16)


def permuted(block, order):
    return dot(block, order).astype(BF16)


def first_block(ret, after, r0_ref, sem):
    copied(ret.at[0], r0_ref, sem)


def own_partials(counts, exc, faces, hist, r0, ret, d0_ref, d1_ref, select_ref, order_ref, r1, sem):
    copy = pltpu.make_async_copy(ret.at[1], r1, sem)
    copy.start()
    width = hist.shape[2]
    col = column_of(lax.broadcasted_iota(jnp.int32, (width, 1), 0))
    first_col = position() * 2
    m0, m1 = live(counts, 0), live(counts, 1)

    def placed(step):
        e = exc[step]
        return jnp.where(col == first_col, e[0:1], jnp.where(col == first_col + 1, e[1:2], 0.0))

    order = permutation(width)
    order_ref[...] = order
    select_ref[...] = one_hot_rows(faces[...], select_ref.shape[0])
    h0, h1 = permuted(hist[0], order), permuted(hist[1], order)
    p0 = dot(r0[...], h0) * m0
    copy.wait()
    p0 += dot(r1[...], h1) * m1
    d0_ref[...] = (placed(0) - p0.T).astype(BF16)
    d1_ref[...] = placed(1) - (dot(r1[...], h0) * m1).T


def pack_partials(counts, order, d0, d1, r0, before, hist, out, h0_ref):
    h0_ref[...] = hist[0]
    n = d0.shape[1]
    out[:, :n] = d0[...]
    p1 = dot(r0[...], permuted(before[...], order[...])) * live(counts, 0)
    out[:, n:] = (d1[...] - p1.T).astype(BF16)


def sum_parts(x, out):
    total = x[0].astype(F32)
    for i in range(1, x.shape[0]):
        total += x[i].astype(F32)
    out[...] = total


def trace_of(first, select, up_ref, down_ref):
    trace = dot(first.astype(BF16), select[...]).astype(BF16)
    half = select.shape[1] // 2
    down_ref[...] = trace[:, :half]
    up_ref[...] = trace[:, half:]


def coupled(up, down, inv, tra):
    half = up.shape[1]
    coupling = dot_t(up[...], tra[:, :half]) + dot_t(down[...], tra[:, half:])
    return dot_t(coupling.astype(BF16), inv[...])


def first_of_sum(x0, x1, x2, x3, inv, select, first_ref, rest_ref, up_ref, down_ref):
    n = inv.shape[0]
    total = (x0[...] + x1[...]) + (x2[...] + x3[...])
    first = dot_t(total[:, :n].astype(BF16), inv[...])
    first_ref[...] = first
    rest_ref[...] = total[:, n:]
    trace_of(first, select, up_ref, down_ref)


def next_first(
    counts, first, rest, up, down, inv, tra, select, r0_even, r0_odd,
    cur_ref, first_ref, up_ref, down_ref,
    r0, sem,
):
    odd = lax.axis_index("c") == 1

    @pl.when(odd)
    def _():
        copied(r0_odd, r0, sem)

    @pl.when(jnp.logical_not(odd))
    def _():
        copied(r0_even, r0, sem)

    cur = first[...] - coupled(up, down, inv, tra)
    cur_ref[...] = cur
    alive = (counts[0] > 0).astype(F32)
    newest = dot_t(cur.astype(BF16), r0[...]) * alive
    following = dot_t((rest[...] - newest).astype(BF16), inv[...])
    first_ref[...] = following
    trace_of(following, select, up_ref, down_ref)


def second_current(cur0, first, up, down, inv, tra, gather_ref, *share_refs):
    cur1 = first[...] - coupled(up, down, inv, tra)
    c0 = cur0[...]
    both = jnp.concatenate([cur1.astype(BF16), c0.astype(BF16)], axis=0)
    for i in range(gather_ref.shape[0]):
        gather_ref[i] = both
    for i, share in enumerate(share_refs):
        share[0] = c0[2 * i : 2 * i + 2]
        share[1] = cur1[2 * i : 2 * i + 2]


def finish(gathered, s0, s1, s2, s3, before0, before1, cur_ref, hist_ref):
    zh = lax.axis_index("zh")
    cur_ref[...] = jnp.where(zh < 2, jnp.where(zh == 0, s0[...], s1[...]), jnp.where(zh == 2, s2[...], s3[...]))
    leading = position() == 0

    @pl.when(leading)
    def _():
        owners, cols = gathered.shape[0], gathered.shape[1] // 2
        order = permutation(owners * cols)
        for slot in range(2):
            both = gathered[:, slot * cols : (slot + 1) * cols, :].reshape(owners * cols, -1)
            hist_ref[slot] = dot_t(both.astype(F32).T.astype(BF16), order).astype(BF16)

    @pl.when(jnp.logical_not(leading))
    def _():
        hist_ref[0] = before0[...]
        hist_ref[1] = before1[...]


def relay(held_at, first_at, held, first, second, after, out, sem):
    y = lax.axis_index("y")
    holds, from_first = one_of(y, held_at), one_of(y, first_at)

    @pl.when(holds)
    def _():
        copied(held, out, sem)

    @pl.when(jnp.logical_and(jnp.logical_not(holds), from_first))
    def _():
        copied(first, out, sem)

    @pl.when(jnp.logical_not(jnp.logical_or(holds, from_first)))
    def _():
        copied(second, out, sem)


def one_of(value, members):
    found = value == members[0]
    for member in members[1:]:
        found = jnp.logical_or(found, value == member)
    return found


def permute(value, axes, pairs):
    return lax.ppermute(value, axes, pairs)


def body(excitation, retarded, history, inverse, transfer, faces, counts):
    slots, n, width = history.shape
    steps = excitation.shape[0]
    half = faces.shape[1] // 2
    devices = Y * ZH * CORE
    cols = width // OWNERS
    exc = jnp.transpose(excitation, (0, 2, 1))
    any_spec = pl.BlockSpec(memory_space=pl.ANY)

    def at(yy, z, c):
        return (yy * ZH + z) * CORE + c

    def spread(value, *hops):
        return permute(value, DELAY, [(at(i, 0, 0), at(j, 0, 0)) for i, j in hops])

    def relayed(held_at, first_at, *operands):
        return call(
            functools.partial(relay, held_at, first_at),
            shape((n, n), BF16),
            [any_spec] * 4,
            0,
            1024 * 1024,
            scratch_shapes=[pltpu.SemaphoreType.DMA],
        )(*operands)

    ring = [(i, (i + 1) % DOM) for i in range(DOM)]
    back = [(j, i) for i, j in ring]
    chain = [(i, i + 1) for i in range(devices - 1)]

    macs = n * n * width
    last = history[slots - 1]
    before1 = permute(last, DELAY, chain)
    r0 = call(
        first_block,
        shape((n, n), BF16),
        [any_spec] * 2,
        0,
        1024 * 1024,
        mib=53,
        scratch_shapes=[pltpu.SemaphoreType.DMA],
    )(retarded, last)
    d0, d1, select, order = call(
        own_partials,
        (shape((width, n), BF16), shape((width, n), F32), shape((n, 2 * half), BF16), shape((width, width), BF16)),
        [SMEM] + [VMEM] * 4 + [any_spec],
        2 * macs * 4,
        2 * 1024 * 1024,
        mib=52,
        scratch_shapes=[pltpu.VMEM((n, n), BF16), pltpu.SemaphoreType.DMA],
    )(counts, exc, faces, history, r0, retarded)
    s1a, s1b = spread(r0, (0, 3)), spread(r0, (0, 5))
    lanes = 2 * n
    packed, h0 = call(
        pack_partials,
        (shape((width, lanes), BF16), shape((n, width), BF16)),
        [SMEM] + [VMEM] * 6,
        2 * macs,
        1024 * 1024,
    )(counts, order, d0, d1, r0, before1, history)
    before0 = permute(h0, DELAY, chain)
    x = lax.all_to_all(packed.reshape(OWNERS, cols, lanes), ("y", "c"), 0, 0, tiled=True)
    r0 = relayed((0,), (3,), r0, s1a, s1b, packed)
    s2a, s2b = spread(r0, (0, 1), (3, 2), (5, 6)), spread(r0, (0, 7), (3, 4))
    x = call(sum_parts, shape((cols, lanes), F32), [VMEM], 0, 512 * 1024)(x)
    xs = [x] + [permute(x, "zh", [(z, 0)]) for z in (1, 3, 2)]

    def halo(up, down):
        return permute(up, ("zh", "dom"), ring), permute(down, ("zh", "dom"), back)

    trace_shape = (shape((cols, half), BF16),) * 2
    first, rest, up, down = call(
        first_of_sum,
        (shape((cols, n), F32), shape((cols, n), F32)) + trace_shape,
        [VMEM] * 6,
        2 * 8 * n * n * 2,
        1024 * 1024,
    )(*xs, inverse, select)
    r0 = relayed((0, 3, 5), (1, 2, 6), r0, s2a, s2b, rest)
    s3 = permute(r0, DELAY, [(at(i, 0, 0), at(i, 0, 1)) for i in range(Y)])
    up, down = halo(up, down)
    cur0, first, up, down = call(
        next_first,
        (shape((cols, n), F32), shape((cols, n), F32)) + trace_shape,
        [SMEM] + [VMEM] * 7 + [any_spec] * 2,
        2 * 8 * n * n * 5,
        2 * 1024 * 1024,
        scratch_shapes=[pltpu.VMEM((n, n), BF16), pltpu.SemaphoreType.DMA],
    )(counts, first, rest, up, down, inverse, transfer, select, r0, s3)
    up, down = halo(up, down)
    gather, *share = call(
        second_current,
        [shape((OWNERS, 2 * cols, n), BF16)] + [shape((steps, 2, n), F32)] * ZH,
        [VMEM] * 6,
        2 * 8 * n * n * 2,
        1024 * 1024,
    )(cur0, first, up, down, inverse, transfer)
    gather = lax.all_to_all(gather, ("y", "c"), 0, 0, tiled=True)
    for z in range(1, ZH):
        share[z] = permute(share[z], DELAY, [(at(i, 0, c), at(i, z, c)) for i in range(Y) for c in range(CORE)])
    currents, new_history = call(
        finish,
        (shape((steps, 2, n), F32), shape(history.shape, BF16)),
        [VMEM] * 7,
        0,
        1024 * 1024,
    )(gather, *share, before0, before1)
    return jnp.transpose(currents, (0, 2, 1)), new_history


def solution(mesh):
    split = Mesh(mesh.devices.reshape(Y, ZH, CORE, DOM), ("y", "zh", "c", "dom"))
    placed = (
        P(None, "dom", DELAY),
        P(DELAY, "dom", None),
        P(DELAY, "dom", None),
        P("dom", None),
        P("dom", None),
        P("dom", None),
        P("dom"),
    )
    return jax.shard_map(
        body,
        mesh=split,
        in_specs=placed,
        out_specs=(P(None, "dom", DELAY), P(DELAY, "dom", None)),
        check_vma=False,
    )
```

```python
import functools

import jax
import jax.numpy as jnp
from jax import lax
from jax.experimental import pallas as pl
from jax.experimental.pallas import tpu as pltpu
from jax.sharding import Mesh, PartitionSpec as P

Y, ZH, CORE, DOM = 8, 4, 2, 8
OWNERS = Y * CORE
DELAY = ("y", "zh", "c")
F32, BF16 = jnp.float32, jnp.bfloat16
VMEM = pl.BlockSpec(memory_space=pltpu.VMEM)
SMEM = pl.BlockSpec(memory_space=pltpu.SMEM)


def call(kernel, out_shape, in_specs, flops, nbytes, mib=32, out_specs=None, **more):
    if out_specs is None:
        out_specs = jax.tree.map(lambda _: VMEM, out_shape)
    return pl.pallas_call(
        kernel,
        out_shape=out_shape,
        in_specs=in_specs,
        out_specs=out_specs,
        compiler_params=pltpu.CompilerParams(vmem_limit_bytes=mib * 1024 * 1024),
        cost_estimate=pl.CostEstimate(flops=flops, bytes_accessed=nbytes, transcendentals=0),
        **more,
    )


def shape(dims, dtype):
    return jax.ShapeDtypeStruct(dims, dtype)


def dot(a, b):
    return jnp.dot(a, b, preferred_element_type=F32)


def dot_t(a, b):
    return lax.dot_general(a, b, (((1,), (1,)), ((), ())), preferred_element_type=F32)


def one_hot_rows(faces, rows):
    ids = lax.broadcasted_iota(jnp.int32, (rows, faces.shape[1]), 0)
    return (ids == faces).astype(F32).astype(BF16)


def position():
    return (lax.axis_index("y") * ZH + lax.axis_index("zh")) * CORE + lax.axis_index("c")


def live(counts, slot):
    return (position() * 2 + slot < counts[0]).astype(F32)


def copied(source, target, sem):
    copy = pltpu.make_async_copy(source, target, sem)
    copy.start()
    copy.wait()


def column_of(row):
    c, zh = (row // 8) % 2, (row // 2) % 4
    return (row // 16) * 16 + zh * 4 + c * 2 + row % 2


def permutation(width):
    cols = lax.broadcasted_iota(jnp.int32, (width, width), 0)
    rows = lax.broadcasted_iota(jnp.int32, (width, width), 1)
    return (cols == column_of(rows)).astype(F32).astype(BF16)


def permuted(block, order):
    return dot(block, order).astype(BF16)


def first_block(ret, after, r0_ref, sem):
    copied(ret.at[0], r0_ref, sem)


def own_partials(counts, exc, faces, hist, r0, ret, d0_ref, d1_ref, select_ref, order_ref, r1, sem):
    copy = pltpu.make_async_copy(ret.at[1], r1, sem)
    copy.start()
    width = hist.shape[2]
    col = column_of(lax.broadcasted_iota(jnp.int32, (width, 1), 0))
    first_col = position() * 2
    m0, m1 = live(counts, 0), live(counts, 1)

    def placed(step):
        e = exc[step]
        return jnp.where(col == first_col, e[0:1], jnp.where(col == first_col + 1, e[1:2], 0.0))

    order = permutation(width)
    order_ref[...] = order
    select_ref[...] = one_hot_rows(faces[...], select_ref.shape[0])
    h0, h1 = permuted(hist[0], order), permuted(hist[1], order)
    p0 = dot(r0[...], h0) * m0
    copy.wait()
    p0 += dot(r1[...], h1) * m1
    d0_ref[...] = (placed(0) - p0.T).astype(BF16)
    d1_ref[...] = placed(1) - (dot(r1[...], h0) * m1).T


def pack_partials(counts, order, d0, d1, r0, before, hist, out, h0_ref):
    h0_ref[...] = hist[0]
    n = d0.shape[1]
    out[:, :n] = d0[...]
    p1 = dot(r0[...], permuted(before[...], order[...])) * live(counts, 0)
    out[:, n:] = (d1[...] - p1.T).astype(BF16)


def sum_parts(x, out):
    total = x[0].astype(F32)
    for i in range(1, x.shape[0]):
        total += x[i].astype(F32)
    out[...] = total


def trace_of(first, select, up_ref, down_ref):
    trace = dot(first.astype(BF16), select[...]).astype(BF16)
    half = select.shape[1] // 2
    down_ref[...] = trace[:, :half]
    up_ref[...] = trace[:, half:]


def coupled(up, down, inv, tra):
    half = up.shape[1]
    coupling = dot_t(up[...], tra[:, :half]) + dot_t(down[...], tra[:, half:])
    return dot_t(coupling.astype(BF16), inv[...])


def first_of_sum(x0, x1, x2, x3, inv, select, first_ref, rest_ref, up_ref, down_ref):
    n = inv.shape[0]
    total = (x0[...] + x1[...]) + (x2[...] + x3[...])
    first = dot_t(total[:, :n].astype(BF16), inv[...])
    first_ref[...] = first
    rest_ref[...] = total[:, n:]
    trace_of(first, select, up_ref, down_ref)


def next_first(
    counts, first, rest, up, down, inv, tra, select, r0_even, r0_odd,
    cur_ref, first_ref, up_ref, down_ref,
    r0, sem,
):
    odd = lax.axis_index("c") == 1

    @pl.when(odd)
    def _():
        pltpu.make_async_copy(r0_odd, r0, sem).start()

    @pl.when(jnp.logical_not(odd))
    def _():
        pltpu.make_async_copy(r0_even, r0, sem).start()

    cur = first[...] - coupled(up, down, inv, tra)
    cur_ref[...] = cur
    alive = (counts[0] > 0).astype(F32)
    pltpu.make_async_copy(r0_even, r0, sem).wait()
    newest = dot_t(cur.astype(BF16), r0[...]) * alive
    following = dot_t((rest[...] - newest).astype(BF16), inv[...])
    first_ref[...] = following
    trace_of(following, select, up_ref, down_ref)


def second_current(cur0, first, up, down, inv, tra, gather_ref, s0, s1, s2, s3, both, sem):
    cur1 = first[...] - coupled(up, down, inv, tra)
    c0 = cur0[...]
    both[...] = jnp.concatenate([cur1.astype(BF16), c0.astype(BF16)], axis=0)
    copy = pltpu.make_async_copy(both, gather_ref.at[0], sem)
    copy.start()
    for i, share in enumerate((s0, s1, s2, s3)):
        share[0] = c0[2 * i : 2 * i + 2]
        share[1] = cur1[2 * i : 2 * i + 2]
    copy.wait()


def finish(gathered, s0, s1, s2, s3, before0, before1, cur_ref, hist_ref):
    zh = lax.axis_index("zh")
    cur_ref[...] = jnp.where(zh < 2, jnp.where(zh == 0, s0[...], s1[...]), jnp.where(zh == 2, s2[...], s3[...]))
    leading = position() == 0

    @pl.when(leading)
    def _():
        owners, cols = gathered.shape[0], gathered.shape[1] // 2
        order = permutation(owners * cols)
        for slot in range(2):
            both = gathered[:, slot * cols : (slot + 1) * cols, :].reshape(owners * cols, -1)
            turned = lax.dot_general(both, order, (((0,), (1,)), ((), ())), preferred_element_type=F32)
            hist_ref[slot] = turned.astype(BF16)

    @pl.when(jnp.logical_not(leading))
    def _():
        hist_ref[0] = before0[...]
        hist_ref[1] = before1[...]


def relay(held_at, first_at, held, first, second, after, out, sem):
    y = lax.axis_index("y")
    holds, from_first = one_of(y, held_at), one_of(y, first_at)

    @pl.when(holds)
    def _():
        copied(held, out, sem)

    @pl.when(jnp.logical_and(jnp.logical_not(holds), from_first))
    def _():
        copied(first, out, sem)

    @pl.when(jnp.logical_not(jnp.logical_or(holds, from_first)))
    def _():
        copied(second, out, sem)


def one_of(value, members):
    found = value == members[0]
    for member in members[1:]:
        found = jnp.logical_or(found, value == member)
    return found


def permute(value, axes, pairs):
    return lax.ppermute(value, axes, pairs)


def body(excitation, retarded, history, inverse, transfer, faces, counts):
    slots, n, width = history.shape
    steps = excitation.shape[0]
    half = faces.shape[1] // 2
    devices = Y * ZH * CORE
    cols = width // OWNERS
    exc = jnp.transpose(excitation, (0, 2, 1))
    any_spec = pl.BlockSpec(memory_space=pl.ANY)

    def at(yy, z, c):
        return (yy * ZH + z) * CORE + c

    def spread(value, *hops):
        return permute(value, DELAY, [(at(i, 0, 0), at(j, 0, 0)) for i, j in hops])

    def relayed(held_at, first_at, *operands):
        return call(
            functools.partial(relay, held_at, first_at),
            shape((n, n), BF16),
            [any_spec] * 4,
            0,
            1024 * 1024,
            scratch_shapes=[pltpu.SemaphoreType.DMA],
        )(*operands)

    ring = [(i, (i + 1) % DOM) for i in range(DOM)]
    back = [(j, i) for i, j in ring]
    chain = [(i, i + 1) for i in range(devices - 1)]

    macs = n * n * width
    last = history[slots - 1]
    before1 = permute(last, DELAY, chain)
    r0 = call(
        first_block,
        shape((n, n), BF16),
        [any_spec] * 2,
        0,
        1024 * 1024,
        mib=53,
        scratch_shapes=[pltpu.SemaphoreType.DMA],
    )(retarded, last)
    d0, d1, select, order = call(
        own_partials,
        (shape((width, n), BF16), shape((width, n), F32), shape((n, 2 * half), BF16), shape((width, width), BF16)),
        [SMEM] + [VMEM] * 4 + [any_spec],
        2 * macs * 4,
        2 * 1024 * 1024,
        mib=52,
        scratch_shapes=[pltpu.VMEM((n, n), BF16), pltpu.SemaphoreType.DMA],
    )(counts, exc, faces, history, r0, retarded)
    s1a, s1b = spread(r0, (0, 3)), spread(r0, (0, 5))
    lanes = 2 * n
    packed, h0 = call(
        pack_partials,
        (shape((width, lanes), BF16), shape((n, width), BF16)),
        [SMEM] + [VMEM] * 6,
        2 * macs,
        1024 * 1024,
    )(counts, order, d0, d1, r0, before1, history)
    before0 = permute(h0, DELAY, chain)
    x = lax.all_to_all(packed.reshape(OWNERS, cols, lanes), ("y", "c"), 0, 0, tiled=True)
    r0 = relayed((0,), (3,), r0, s1a, s1b, packed)
    s2a, s2b = spread(r0, (0, 1), (3, 2), (5, 6)), spread(r0, (0, 7), (3, 4))
    x = call(sum_parts, shape((cols, lanes), F32), [VMEM], 0, 512 * 1024)(x)
    xs = [x] + [permute(x, "zh", [(z, 0)]) for z in (1, 3, 2)]

    def halo(up, down):
        return permute(up, ("zh", "dom"), ring), permute(down, ("zh", "dom"), back)

    trace_shape = (shape((cols, half), BF16),) * 2
    first, rest, up, down = call(
        first_of_sum,
        (shape((cols, n), F32), shape((cols, n), F32)) + trace_shape,
        [VMEM] * 6,
        2 * 8 * n * n * 2,
        1024 * 1024,
    )(*xs, inverse, select)
    r0 = relayed((0, 3, 5), (1, 2, 6), r0, s2a, s2b, rest)
    s3 = permute(r0, DELAY, [(at(i, 0, 0), at(i, 0, 1)) for i in range(Y)])
    up, down = halo(up, down)
    cur0, first, up, down = call(
        next_first,
        (shape((cols, n), F32), shape((cols, n), F32)) + trace_shape,
        [SMEM] + [VMEM] * 7 + [any_spec] * 2,
        2 * 8 * n * n * 5,
        2 * 1024 * 1024,
        scratch_shapes=[pltpu.VMEM((n, n), BF16), pltpu.SemaphoreType.DMA],
    )(counts, first, rest, up, down, inverse, transfer, select, r0, s3)
    up, down = halo(up, down)
    gather, *share = call(
        second_current,
        [shape((OWNERS, 2 * cols, n), BF16)] + [shape((steps, 2, n), F32)] * ZH,
        [VMEM] * 6,
        2 * 8 * n * n * 2,
        1024 * 1024,
        out_specs=[any_spec] + [VMEM] * ZH,
        scratch_shapes=[pltpu.VMEM((2 * cols, n), BF16), pltpu.SemaphoreType.DMA],
    )(cur0, first, up, down, inverse, transfer)
    gather = lax.all_to_all(gather, ("y", "c"), 0, 0, tiled=True)
    for z in range(1, ZH):
        share[z] = permute(share[z], DELAY, [(at(i, 0, c), at(i, z, c)) for i in range(Y) for c in range(CORE)])
    currents, new_history = call(
        finish,
        (shape((steps, 2, n), F32), shape(history.shape, BF16)),
        [VMEM] * 7,
        0,
        1024 * 1024,
    )(gather, *share, before0, before1)
    return jnp.transpose(currents, (0, 2, 1)), new_history


def solution(mesh):
    split = Mesh(mesh.devices.reshape(Y, ZH, CORE, DOM), ("y", "zh", "c", "dom"))
    placed = (
        P(None, "dom", DELAY),
        P(DELAY, "dom", None),
        P(DELAY, "dom", None),
        P("dom", None),
        P("dom", None),
        P("dom", None),
        P("dom"),
    )
    return jax.shard_map(
        body,
        mesh=split,
        in_specs=placed,
        out_specs=(P(None, "dom", DELAY), P(DELAY, "dom", None)),
        check_vma=False,
    )
```

```python
import functools

import jax
import jax.numpy as jnp
from jax import lax
from jax.experimental import pallas as pl
from jax.experimental.pallas import tpu as pltpu
from jax.sharding import Mesh, PartitionSpec as P

Y, ZH, CORE, DOM = 8, 4, 2, 8
OWNERS = Y * CORE
DELAY = ("y", "zh", "c")
F32, BF16 = jnp.float32, jnp.bfloat16
VMEM = pl.BlockSpec(memory_space=pltpu.VMEM)
SMEM = pl.BlockSpec(memory_space=pltpu.SMEM)


def call(kernel, out_shape, in_specs, flops, nbytes, mib=32, out_specs=None, **more):
    if out_specs is None:
        out_specs = jax.tree.map(lambda _: VMEM, out_shape)
    return pl.pallas_call(
        kernel,
        out_shape=out_shape,
        in_specs=in_specs,
        out_specs=out_specs,
        compiler_params=pltpu.CompilerParams(vmem_limit_bytes=mib * 1024 * 1024),
        cost_estimate=pl.CostEstimate(flops=flops, bytes_accessed=nbytes, transcendentals=0),
        **more,
    )


def shape(dims, dtype):
    return jax.ShapeDtypeStruct(dims, dtype)


def dot(a, b):
    return jnp.dot(a, b, preferred_element_type=F32)


def dot_t(a, b):
    return lax.dot_general(a, b, (((1,), (1,)), ((), ())), preferred_element_type=F32)


def one_hot_rows(faces, rows):
    ids = lax.broadcasted_iota(jnp.int32, (rows, faces.shape[1]), 0)
    return (ids == faces).astype(F32).astype(BF16)


def position():
    return (lax.axis_index("y") * ZH + lax.axis_index("zh")) * CORE + lax.axis_index("c")


def live(counts, slot):
    return (position() * 2 + slot < counts[0]).astype(F32)


def copied(source, target, sem):
    copy = pltpu.make_async_copy(source, target, sem)
    copy.start()
    copy.wait()


def column_of(row):
    c, zh = (row // 8) % 2, (row // 2) % 4
    return (row // 16) * 16 + zh * 4 + c * 2 + row % 2


def permutation(width):
    cols = lax.broadcasted_iota(jnp.int32, (width, width), 0)
    rows = lax.broadcasted_iota(jnp.int32, (width, width), 1)
    return (cols == column_of(rows)).astype(F32).astype(BF16)


def permuted(block, order):
    return dot(block, order).astype(BF16)


def first_block(ret, after, r0_ref, sem):
    copied(ret.at[0], r0_ref, sem)


def own_partials(counts, exc, faces, hist, r0, ret, d0_ref, d1_ref, select_ref, order_ref, r1, sem):
    copy = pltpu.make_async_copy(ret.at[1], r1, sem)
    copy.start()
    width = hist.shape[2]
    col = column_of(lax.broadcasted_iota(jnp.int32, (width, 1), 0))
    first_col = position() * 2
    m0, m1 = live(counts, 0), live(counts, 1)

    def placed(step):
        e = exc[step]
        return jnp.where(col == first_col, e[0:1], jnp.where(col == first_col + 1, e[1:2], 0.0))

    order = permutation(width)
    order_ref[...] = order
    select_ref[...] = one_hot_rows(faces[...], select_ref.shape[0])
    h0, h1 = permuted(hist[0], order), permuted(hist[1], order)
    p0 = dot(r0[...], h0) * m0
    copy.wait()
    p0 += dot(r1[...], h1) * m1
    d0_ref[...] = (placed(0) - p0.T).astype(BF16)
    d1_ref[...] = placed(1) - (dot(r1[...], h0) * m1).T


def pack_partials(counts, order, d0, d1, r0, before, hist, out, h0_ref):
    h0_ref[...] = hist[0]
    n = d0.shape[1]
    out[:, :n] = d0[...]
    p1 = dot(r0[...], permuted(before[...], order[...])) * live(counts, 0)
    out[:, n:] = (d1[...] - p1.T).astype(BF16)


def sum_parts(x, out):
    total = x[0].astype(F32)
    for i in range(1, x.shape[0]):
        total += x[i].astype(F32)
    out[...] = total


def trace_of(first, select, up_ref, down_ref):
    trace = dot(first.astype(BF16), select[...]).astype(BF16)
    half = select.shape[1] // 2
    down_ref[...] = trace[:, :half]
    up_ref[...] = trace[:, half:]


def coupled(up, down, inv, tra):
    half = up.shape[1]
    coupling = dot_t(up[...], tra[:, :half]) + dot_t(down[...], tra[:, half:])
    return dot_t(coupling.astype(BF16), inv[...])


def first_of_sum(x0, x1, x2, x3, inv, select, first_ref, rest_ref, up_ref, down_ref):
    n = inv.shape[0]
    total = (x0[...] + x1[...]) + (x2[...] + x3[...])
    first = dot_t(total[:, :n].astype(BF16), inv[...])
    first_ref[...] = first
    rest_ref[...] = total[:, n:]
    trace_of(first, select, up_ref, down_ref)


def next_first(
    counts, first, rest, up, down, inv, tra, select, r0_even, r0_odd,
    cur_ref, first_ref, traces_ref,
    r0, sem,
):
    odd = lax.axis_index("c") == 1

    @pl.when(odd)
    def _():
        pltpu.make_async_copy(r0_odd, r0, sem).start()

    @pl.when(jnp.logical_not(odd))
    def _():
        pltpu.make_async_copy(r0_even, r0, sem).start()

    cur = first[...] - coupled(up, down, inv, tra)
    cur_ref[...] = cur
    alive = (counts[0] > 0).astype(F32)
    pltpu.make_async_copy(r0_even, r0, sem).wait()
    newest = dot_t(cur.astype(BF16), r0[...]) * alive
    following = dot_t((rest[...] - newest).astype(BF16), inv[...])
    first_ref[...] = following
    half = select.shape[1] // 2
    trace = dot(following.astype(BF16), select[...]).astype(BF16)
    dom = lax.axis_index("dom")
    traces_ref[...] = jnp.zeros_like(traces_ref)
    traces_ref[(dom + 1) % DOM] = trace[:, half:]
    traces_ref[(dom + DOM - 1) % DOM] = trace[:, :half]


def second_current(cur0, first, traces, inv, tra, gather_ref, s0, s1, s2, s3, both, sem):
    dom = lax.axis_index("dom")
    up, down = traces[(dom + DOM - 1) % DOM], traces[(dom + 1) % DOM]
    cur1 = first[...] - coupled(up, down, inv, tra)
    c0 = cur0[...]
    both[...] = jnp.concatenate([cur1.astype(BF16), c0.astype(BF16)], axis=0)
    copy = pltpu.make_async_copy(both, gather_ref.at[0], sem)
    copy.start()
    for i, share in enumerate((s0, s1, s2, s3)):
        share[0] = c0[2 * i : 2 * i + 2]
        share[1] = cur1[2 * i : 2 * i + 2]
    copy.wait()


def finish(gathered, s0, s1, s2, s3, before0, before1, cur_ref, hist_ref):
    zh = lax.axis_index("zh")
    cur_ref[...] = jnp.where(zh < 2, jnp.where(zh == 0, s0[...], s1[...]), jnp.where(zh == 2, s2[...], s3[...]))
    leading = position() == 0

    @pl.when(leading)
    def _():
        owners, cols = gathered.shape[0], gathered.shape[1] // 2
        order = permutation(owners * cols)
        for slot in range(2):
            both = gathered[:, slot * cols : (slot + 1) * cols, :].reshape(owners * cols, -1)
            turned = lax.dot_general(both, order, (((0,), (1,)), ((), ())), preferred_element_type=F32)
            hist_ref[slot] = turned.astype(BF16)

    @pl.when(jnp.logical_not(leading))
    def _():
        hist_ref[0] = before0[...]
        hist_ref[1] = before1[...]


def relay(held_at, first_at, held, first, second, after, out, sem):
    y = lax.axis_index("y")
    holds, from_first = one_of(y, held_at), one_of(y, first_at)

    @pl.when(holds)
    def _():
        copied(held, out, sem)

    @pl.when(jnp.logical_and(jnp.logical_not(holds), from_first))
    def _():
        copied(first, out, sem)

    @pl.when(jnp.logical_not(jnp.logical_or(holds, from_first)))
    def _():
        copied(second, out, sem)


def one_of(value, members):
    found = value == members[0]
    for member in members[1:]:
        found = jnp.logical_or(found, value == member)
    return found


def permute(value, axes, pairs):
    return lax.ppermute(value, axes, pairs)


def body(excitation, retarded, history, inverse, transfer, faces, counts):
    slots, n, width = history.shape
    steps = excitation.shape[0]
    half = faces.shape[1] // 2
    devices = Y * ZH * CORE
    cols = width // OWNERS
    exc = jnp.transpose(excitation, (0, 2, 1))
    any_spec = pl.BlockSpec(memory_space=pl.ANY)

    def at(yy, z, c):
        return (yy * ZH + z) * CORE + c

    def spread(value, *hops):
        return permute(value, DELAY, [(at(i, 0, 0), at(j, 0, 0)) for i, j in hops])

    def relayed(held_at, first_at, *operands):
        return call(
            functools.partial(relay, held_at, first_at),
            shape((n, n), BF16),
            [any_spec] * 4,
            0,
            1024 * 1024,
            scratch_shapes=[pltpu.SemaphoreType.DMA],
        )(*operands)

    ring = [(i, (i + 1) % DOM) for i in range(DOM)]
    back = [(j, i) for i, j in ring]
    chain = [(i, i + 1) for i in range(devices - 1)]

    macs = n * n * width
    last = history[slots - 1]
    before1 = permute(last, DELAY, chain)
    r0 = call(
        first_block,
        shape((n, n), BF16),
        [any_spec] * 2,
        0,
        1024 * 1024,
        mib=53,
        scratch_shapes=[pltpu.SemaphoreType.DMA],
    )(retarded, last)
    d0, d1, select, order = call(
        own_partials,
        (shape((width, n), BF16), shape((width, n), F32), shape((n, 2 * half), BF16), shape((width, width), BF16)),
        [SMEM] + [VMEM] * 4 + [any_spec],
        2 * macs * 4,
        2 * 1024 * 1024,
        mib=52,
        scratch_shapes=[pltpu.VMEM((n, n), BF16), pltpu.SemaphoreType.DMA],
    )(counts, exc, faces, history, r0, retarded)
    s1a, s1b = spread(r0, (0, 3)), spread(r0, (0, 5))
    lanes = 2 * n
    packed, h0 = call(
        pack_partials,
        (shape((width, lanes), BF16), shape((n, width), BF16)),
        [SMEM] + [VMEM] * 6,
        2 * macs,
        1024 * 1024,
    )(counts, order, d0, d1, r0, before1, history)
    before0 = permute(h0, DELAY, chain)
    x = lax.all_to_all(packed.reshape(OWNERS, cols, lanes), ("y", "c"), 0, 0, tiled=True)
    r0 = relayed((0,), (3,), r0, s1a, s1b, packed)
    s2a, s2b = spread(r0, (0, 1), (3, 2), (5, 6)), spread(r0, (0, 7), (3, 4))
    x = call(sum_parts, shape((cols, lanes), F32), [VMEM], 0, 512 * 1024)(x)
    xs = [x] + [permute(x, "zh", [(z, 0)]) for z in (1, 3, 2)]

    def halo(up, down):
        return permute(up, ("zh", "dom"), ring), permute(down, ("zh", "dom"), back)

    trace_shape = (shape((cols, half), BF16),) * 2
    first, rest, up, down = call(
        first_of_sum,
        (shape((cols, n), F32), shape((cols, n), F32)) + trace_shape,
        [VMEM] * 6,
        2 * 8 * n * n * 2,
        1024 * 1024,
    )(*xs, inverse, select)
    r0 = relayed((0, 3, 5), (1, 2, 6), r0, s2a, s2b, rest)
    s3 = permute(r0, DELAY, [(at(i, 0, 0), at(i, 0, 1)) for i in range(Y)])
    up, down = halo(up, down)
    cur0, first, traces = call(
        next_first,
        (shape((cols, n), F32), shape((cols, n), F32), shape((DOM, cols, half), BF16)),
        [SMEM] + [VMEM] * 7 + [any_spec] * 2,
        2 * 8 * n * n * 5,
        2 * 1024 * 1024,
        scratch_shapes=[pltpu.VMEM((n, n), BF16), pltpu.SemaphoreType.DMA],
    )(counts, first, rest, up, down, inverse, transfer, select, r0, s3)
    traces = lax.all_to_all(traces, "dom", 0, 0, tiled=True)
    gather, *share = call(
        second_current,
        [shape((OWNERS, 2 * cols, n), BF16)] + [shape((steps, 2, n), F32)] * ZH,
        [VMEM] * 5,
        2 * 8 * n * n * 2,
        1024 * 1024,
        out_specs=[any_spec] + [VMEM] * ZH,
        scratch_shapes=[pltpu.VMEM((2 * cols, n), BF16), pltpu.SemaphoreType.DMA],
    )(cur0, first, traces, inverse, transfer)
    gather = lax.all_to_all(gather, ("y", "c"), 0, 0, tiled=True)
    for z in range(1, ZH):
        share[z] = permute(share[z], DELAY, [(at(i, 0, c), at(i, z, c)) for i in range(Y) for c in range(CORE)])
    currents, new_history = call(
        finish,
        (shape((steps, 2, n), F32), shape(history.shape, BF16)),
        [VMEM] * 7,
        0,
        1024 * 1024,
    )(gather, *share, before0, before1)
    return jnp.transpose(currents, (0, 2, 1)), new_history


def solution(mesh):
    split = Mesh(mesh.devices.reshape(Y, ZH, CORE, DOM), ("y", "zh", "c", "dom"))
    placed = (
        P(None, "dom", DELAY),
        P(DELAY, "dom", None),
        P(DELAY, "dom", None),
        P("dom", None),
        P("dom", None),
        P("dom", None),
        P("dom"),
    )
    return jax.shard_map(
        body,
        mesh=split,
        in_specs=placed,
        out_specs=(P(None, "dom", DELAY), P(DELAY, "dom", None)),
        check_vma=False,
    )
```

```python
import functools

import jax
import jax.numpy as jnp
from jax import lax
from jax.experimental import pallas as pl
from jax.experimental.pallas import tpu as pltpu
from jax.sharding import Mesh, PartitionSpec as P

Y, ZH, CORE, DOM = 8, 4, 2, 8
OWNERS = Y * CORE
DELAY = ("y", "zh", "c")
F32, BF16 = jnp.float32, jnp.bfloat16
VMEM = pl.BlockSpec(memory_space=pltpu.VMEM)
SMEM = pl.BlockSpec(memory_space=pltpu.SMEM)


def call(kernel, out_shape, in_specs, flops, nbytes, mib=32, out_specs=None, **more):
    if out_specs is None:
        out_specs = jax.tree.map(lambda _: VMEM, out_shape)
    return pl.pallas_call(
        kernel,
        out_shape=out_shape,
        in_specs=in_specs,
        out_specs=out_specs,
        compiler_params=pltpu.CompilerParams(vmem_limit_bytes=mib * 1024 * 1024),
        cost_estimate=pl.CostEstimate(flops=flops, bytes_accessed=nbytes, transcendentals=0),
        **more,
    )


def shape(dims, dtype):
    return jax.ShapeDtypeStruct(dims, dtype)


def dot(a, b):
    return jnp.dot(a, b, preferred_element_type=F32)


def dot_t(a, b):
    return lax.dot_general(a, b, (((1,), (1,)), ((), ())), preferred_element_type=F32)


def one_hot_rows(faces, rows):
    ids = lax.broadcasted_iota(jnp.int32, (rows, faces.shape[1]), 0)
    return (ids == faces).astype(F32).astype(BF16)


def position():
    return (lax.axis_index("y") * ZH + lax.axis_index("zh")) * CORE + lax.axis_index("c")


def live(counts, slot):
    return (position() * 2 + slot < counts[0]).astype(F32)


def copied(source, target, sem):
    copy = pltpu.make_async_copy(source, target, sem)
    copy.start()
    copy.wait()


def column_of(row):
    c, zh = (row // 8) % 2, (row // 2) % 4
    return (row // 16) * 16 + zh * 4 + c * 2 + row % 2


def permutation(width):
    cols = lax.broadcasted_iota(jnp.int32, (width, width), 0)
    rows = lax.broadcasted_iota(jnp.int32, (width, width), 1)
    return (cols == column_of(rows)).astype(F32).astype(BF16)


def permuted(block, order):
    return dot(block, order).astype(BF16)


def first_block(ret, after, r0_ref, sem):
    copied(ret.at[0], r0_ref, sem)


def own_partials(counts, exc, faces, hist, r0, ret, d0_ref, d1_ref, select_ref, order_ref, r1, sem):
    copy = pltpu.make_async_copy(ret.at[1], r1, sem)
    copy.start()
    width = hist.shape[2]
    col = column_of(lax.broadcasted_iota(jnp.int32, (width, 1), 0))
    first_col = position() * 2
    m0, m1 = live(counts, 0), live(counts, 1)

    def placed(step):
        e = exc[step]
        return jnp.where(col == first_col, e[0:1], jnp.where(col == first_col + 1, e[1:2], 0.0))

    order = permutation(width)
    order_ref[...] = order
    select_ref[...] = one_hot_rows(faces[...], select_ref.shape[0])
    h0, h1 = permuted(hist[0], order), permuted(hist[1], order)
    p0 = dot(r0[...], h0) * m0
    copy.wait()
    p0 += dot(r1[...], h1) * m1
    d0_ref[...] = (placed(0) - p0.T).astype(BF16)
    d1_ref[...] = placed(1) - (dot(r1[...], h0) * m1).T


def pack_partials(counts, order, d0, d1, r0, before, hist, out, h0_ref):
    h0_ref[...] = hist[0]
    n = d0.shape[1]
    out[:, :n] = d0[...]
    p1 = dot(r0[...], permuted(before[...], order[...])) * live(counts, 0)
    out[:, n:] = (d1[...] - p1.T).astype(BF16)


def sum_parts(x, out):
    total = x[0].astype(F32)
    for i in range(1, x.shape[0]):
        total += x[i].astype(F32)
    out[...] = total


def trace_of(first, select, up_ref, down_ref):
    trace = dot(first.astype(BF16), select[...]).astype(BF16)
    half = select.shape[1] // 2
    down_ref[...] = trace[:, :half]
    up_ref[...] = trace[:, half:]


def coupled(up, down, inv, tra):
    half = up.shape[1]
    coupling = dot_t(up[...], tra[:, :half]) + dot_t(down[...], tra[:, half:])
    return dot_t(coupling.astype(BF16), inv[...])


def first_of_sum(x0, x1, x2, x3, inv, select, first_ref, rest_ref, up_ref, down_ref):
    n = inv.shape[0]
    total = (x0[...] + x1[...]) + (x2[...] + x3[...])
    first = dot_t(total[:, :n].astype(BF16), inv[...])
    first_ref[...] = first
    rest_ref[...] = total[:, n:]
    trace_of(first, select, up_ref, down_ref)


def next_first(
    counts, first, rest, up, down, inv, tra, select, r0_even, r0_odd,
    cur_ref, first_ref, up_ref, down_ref,
    r0, sem,
):
    odd = lax.axis_index("c") == 1

    @pl.when(odd)
    def _():
        pltpu.make_async_copy(r0_odd, r0, sem).start()

    @pl.when(jnp.logical_not(odd))
    def _():
        pltpu.make_async_copy(r0_even, r0, sem).start()

    cur = first[...] - coupled(up, down, inv, tra)
    cur_ref[...] = cur
    alive = (counts[0] > 0).astype(F32)
    pltpu.make_async_copy(r0_even, r0, sem).wait()
    newest = dot_t(cur.astype(BF16), r0[...]) * alive
    following = dot_t((rest[...] - newest).astype(BF16), inv[...])
    first_ref[...] = following
    trace_of(following, select, up_ref, down_ref)


def second_current(cur0, first, up, down, inv, tra, gather_ref, s0, s1, s2, s3, both, sem):
    cur1 = first[...] - coupled(up, down, inv, tra)
    c0 = cur0[...]
    both[...] = jnp.concatenate([cur1.astype(BF16), c0.astype(BF16)], axis=0)
    copy = pltpu.make_async_copy(both, gather_ref.at[0], sem)
    copy.start()
    for i, share in enumerate((s0, s1, s2, s3)):
        share[0] = c0[2 * i : 2 * i + 2]
        share[1] = cur1[2 * i : 2 * i + 2]
    copy.wait()


def finish(gathered, s0, s1, s2, s3, before0, before1, cur_ref, hist_ref):
    zh = lax.axis_index("zh")
    cur_ref[...] = jnp.where(zh < 2, jnp.where(zh == 0, s0[...], s1[...]), jnp.where(zh == 2, s2[...], s3[...]))
    leading = position() == 0

    @pl.when(leading)
    def _():
        owners, cols = gathered.shape[0], gathered.shape[1] // 2
        order = permutation(owners * cols)
        for slot in range(2):
            both = gathered[:, slot * cols : (slot + 1) * cols, :].reshape(owners * cols, -1)
            turned = lax.dot_general(both, order, (((0,), (1,)), ((), ())), preferred_element_type=F32)
            hist_ref[slot] = turned.astype(BF16)

    @pl.when(jnp.logical_not(leading))
    def _():
        hist_ref[0] = before0[...]
        hist_ref[1] = before1[...]


def relay(members, *refs):
    *sources, after, out, sem = refs
    y = lax.axis_index("y")
    for held_at, source in zip(members, sources):
        @pl.when(one_of(y, held_at))
        def _(source=source):
            copied(source, out, sem)


def one_of(value, members):
    found = value == members[0]
    for member in members[1:]:
        found = jnp.logical_or(found, value == member)
    return found


def permute(value, axes, pairs):
    return lax.ppermute(value, axes, pairs)


def body(excitation, retarded, history, inverse, transfer, faces, counts):
    slots, n, width = history.shape
    steps = excitation.shape[0]
    half = faces.shape[1] // 2
    devices = Y * ZH * CORE
    cols = width // OWNERS
    exc = jnp.transpose(excitation, (0, 2, 1))
    any_spec = pl.BlockSpec(memory_space=pl.ANY)

    def at(yy, z, c):
        return (yy * ZH + z) * CORE + c

    def spread(value, *hops):
        return permute(value, DELAY, [(at(i, 0, 0), at(j, 0, 0)) for i, j in hops])

    def relayed(members, *operands):
        return call(
            functools.partial(relay, members),
            shape((n, n), BF16),
            [any_spec] * len(operands),
            0,
            1024 * 1024,
            scratch_shapes=[pltpu.SemaphoreType.DMA],
        )(*operands)

    ring = [(i, (i + 1) % DOM) for i in range(DOM)]
    back = [(j, i) for i, j in ring]
    chain = [(i, i + 1) for i in range(devices - 1)]

    macs = n * n * width
    last = history[slots - 1]
    before1 = permute(last, DELAY, chain)
    r0 = call(
        first_block,
        shape((n, n), BF16),
        [any_spec] * 2,
        0,
        1024 * 1024,
        mib=53,
        scratch_shapes=[pltpu.SemaphoreType.DMA],
    )(retarded, last)
    d0, d1, select, order = call(
        own_partials,
        (shape((width, n), BF16), shape((width, n), F32), shape((n, 2 * half), BF16), shape((width, width), BF16)),
        [SMEM] + [VMEM] * 4 + [any_spec],
        2 * macs * 4,
        2 * 1024 * 1024,
        mib=52,
        scratch_shapes=[pltpu.VMEM((n, n), BF16), pltpu.SemaphoreType.DMA],
    )(counts, exc, faces, history, r0, retarded)
    s1 = spread(r0, (0, 4))
    lanes = 2 * n
    packed, h0 = call(
        pack_partials,
        (shape((width, lanes), BF16), shape((n, width), BF16)),
        [SMEM] + [VMEM] * 6,
        2 * macs,
        1024 * 1024,
    )(counts, order, d0, d1, r0, before1, history)
    before0 = permute(h0, DELAY, chain)
    x = lax.all_to_all(packed.reshape(OWNERS, cols, lanes), ("y", "c"), 0, 0, tiled=True)
    r0 = relayed(((0, 1, 2, 3), (4, 5, 6, 7)), r0, s1, packed)
    s2 = [spread(r0, (0, k), (4, (4 + k) % Y)) for k in (1, 7, 2)]
    x = call(sum_parts, shape((cols, lanes), F32), [VMEM], 0, 512 * 1024)(x)
    xs = [x] + [permute(x, "zh", [(z, 0)]) for z in (1, 3, 2)]

    def halo(up, down):
        return permute(up, ("zh", "dom"), ring), permute(down, ("zh", "dom"), back)

    trace_shape = (shape((cols, half), BF16),) * 2
    first, rest, up, down = call(
        first_of_sum,
        (shape((cols, n), F32), shape((cols, n), F32)) + trace_shape,
        [VMEM] * 6,
        2 * 8 * n * n * 2,
        1024 * 1024,
    )(*xs, inverse, select)
    r0 = relayed(((0, 4), (1, 5), (7, 3), (2, 6)), r0, *s2, rest)
    s3 = permute(r0, DELAY, [(at(i, 0, 0), at(i, 0, 1)) for i in range(Y)])
    up, down = halo(up, down)
    cur0, first, up, down = call(
        next_first,
        (shape((cols, n), F32), shape((cols, n), F32)) + trace_shape,
        [SMEM] + [VMEM] * 7 + [any_spec] * 2,
        2 * 8 * n * n * 5,
        2 * 1024 * 1024,
        scratch_shapes=[pltpu.VMEM((n, n), BF16), pltpu.SemaphoreType.DMA],
    )(counts, first, rest, up, down, inverse, transfer, select, r0, s3)
    up, down = halo(up, down)
    gather, *share = call(
        second_current,
        [shape((OWNERS, 2 * cols, n), BF16)] + [shape((steps, 2, n), F32)] * ZH,
        [VMEM] * 6,
        2 * 8 * n * n * 2,
        1024 * 1024,
        out_specs=[any_spec] + [VMEM] * ZH,
        scratch_shapes=[pltpu.VMEM((2 * cols, n), BF16), pltpu.SemaphoreType.DMA],
    )(cur0, first, up, down, inverse, transfer)
    gather = lax.all_to_all(gather, ("y", "c"), 0, 0, tiled=True)
    for z in range(1, ZH):
        share[z] = permute(share[z], DELAY, [(at(i, 0, c), at(i, z, c)) for i in range(Y) for c in range(CORE)])
    currents, new_history = call(
        finish,
        (shape((steps, 2, n), F32), shape(history.shape, BF16)),
        [VMEM] * 7,
        0,
        1024 * 1024,
    )(gather, *share, before0, before1)
    return jnp.transpose(currents, (0, 2, 1)), new_history


def solution(mesh):
    split = Mesh(mesh.devices.reshape(Y, ZH, CORE, DOM), ("y", "zh", "c", "dom"))
    placed = (
        P(None, "dom", DELAY),
        P(DELAY, "dom", None),
        P(DELAY, "dom", None),
        P("dom", None),
        P("dom", None),
        P("dom", None),
        P("dom"),
    )
    return jax.shard_map(
        body,
        mesh=split,
        in_specs=placed,
        out_specs=(P(None, "dom", DELAY), P(DELAY, "dom", None)),
        check_vma=False,
    )
```
